128 devices in a mesh: ctx: 16 (over x, y), ch: 8 (over z, core).
Axes of the slice: x: 4, y: 4, z: 4, core: 2. Of those that a mesh axis runs over, the one named last changes fastest.
Arguments:
- inputs: bfloat16 [32768, 4096], P('ctx', 'ch'), may hold values from -6 to 6
- grad_out: bfloat16 [32768, 4096], P('ctx', 'ch'), may hold values from -6 to 6
- residues: float32 [4096, 16], P('ch'), may hold values from -4 to 4
- log_rates: float32 [4096, 16], P('ch'), may hold values from -14 to -2.99
- skip_weight: float32 [4096], P('ch'), may hold values from -4 to 4
Outputs:
- grad_inputs: bfloat16 [32768, 4096], P('ctx', 'ch')
- grad_residues: float32 [4096, 16], P('ch')
- grad_log_rates: float32 [4096, 16], P('ch')
- grad_skip_weight: float32 [4096], P('ch')
The draws below stay inside these ranges and needn't reach their ends.
All inputs are finite; a program needn't handle non-finite values.
Results may differ from the reference program's by a relative error of at most 0.0055.
Values may be sent and summed in bfloat16 or wider, within the bound.
No kernel may reach another device: no remote copies, remote signals or barrier semaphores. Data moves between devices by JAX's collectives and lax.ppermute only.
A program may use at most 128 MiB of HBM per device.

```python
import math
import jax
import jax.numpy as jnp
from jax import lax

C = 4096
MODES = 16
TOKENS = 32768


def draw_log_rates(key, part):
    key = jax.random.fold_in(key, 11)
    key_pick, key_slow, key_fast = jax.random.split(key, 3)
    share = 0.5
    lowest = math.log(0.3 / TOKENS)
    middle = math.log(2.3 / TOKENS)
    highest = math.log(0.05)
    picked = jax.random.uniform(key_pick, (C, MODES), jnp.float32) < share
    slow_part = lowest + jax.random.uniform(key_slow, (C, MODES), jnp.float32) * (middle - lowest)
    fast_part = middle + jax.random.uniform(key_fast, (C, MODES), jnp.float32) * (highest - middle)
    return jnp.where(picked, slow_part, fast_part).astype(jnp.float32)


def block_levels(key, shape, cuts, smallest, largest):
    gain, own = 1.0, jax.random.fold_in(key, 6)
    for dim, blocks in cuts:
        steps = jnp.exp(jax.random.uniform(jax.random.fold_in(own, dim), (blocks,), jnp.float32, smallest / len(cuts), largest / len(cuts)))
        gain = gain * jnp.repeat(steps, shape[dim] // blocks).reshape([-1 if axis == dim else 1 for axis in range(len(shape))])
    return gain


def gaussian(stream_key, dims, scale, reach, cuts=(), kind=jnp.bfloat16):
    loudness = block_levels(stream_key, dims, cuts, -0.22, 0.18) if cuts else 1.0
    values = jax.random.normal(stream_key, dims, jnp.float32) * scale * loudness
    return jnp.minimum(jnp.maximum(values, -reach), reach).astype(kind)


def setup_inputs(seed: int = 0) -> dict:
    key_of = jax.random.split(jax.random.key(seed), 6)
    return {
        "inputs": gaussian(key_of[0], (TOKENS, C), 1.0, 6.0, ((0, 16), (1, 8))),
        "grad_out": gaussian(key_of[1], (TOKENS, C), 1.0, 6.0, ((0, 16), (1, 8))),
        "residues": gaussian(key_of[2], (C, MODES), 1.0, 4.0, ((0, 8),), jnp.float32),
        "log_rates": draw_log_rates(jax.random.fold_in(key_of[5], 71), 0),
        "skip_weight": gaussian(key_of[4], (C,), 1.0, 4.0, ((0, 8),), jnp.float32),
    }


def reference(inputs, grad_out, residues, log_rates, skip_weight):
    length = TOKENS
    padded = 2 * length
    group_width = math.gcd(C, 256)
    group_count = C // group_width
    position = jnp.arange(length, dtype=jnp.float32)
    rates = jnp.exp(log_rates)
    weights = 0.25 * residues * jnp.sqrt(rates)

    def one_group(number):
        offset = (number * group_width).astype(jnp.int32)
        signal = lax.dynamic_slice_in_dim(inputs, offset, group_width, 1).astype(jnp.float32).T
        upstream = lax.dynamic_slice_in_dim(grad_out, offset, group_width, 1).astype(jnp.float32).T
        group_rates = lax.dynamic_slice_in_dim(rates, offset, group_width, 0)
        group_weights = lax.dynamic_slice_in_dim(weights, offset, group_width, 0)
        impulse = jnp.zeros((group_width, length), jnp.float32)
        for mode_index in range(MODES):
            impulse = impulse + group_weights[:, mode_index:mode_index + 1] * jnp.exp(-group_rates[:, mode_index:mode_index + 1] * position[None, :])
        input_spec = jnp.fft.rfft(signal, padded, axis=1)
        grad_spec = jnp.fft.rfft(upstream, padded, axis=1)
        impulse_spec = jnp.fft.rfft(impulse, padded, axis=1)
        lagged = jnp.fft.irfft(grad_spec * jnp.conj(input_spec), padded, axis=1)[:, :length]
        backward = jnp.fft.irfft(grad_spec * jnp.conj(impulse_spec), padded, axis=1)[:, :length]
        first_cols = []
        second_cols = []
        for mode_index in range(MODES):
            decays = jnp.exp(-group_rates[:, mode_index:mode_index + 1] * position[None, :])
            first_cols.append(lax.optimization_barrier(jnp.sum(decays * lagged, axis=1)))
            second_cols.append(lax.optimization_barrier(jnp.sum(position[None, :] * decays * lagged, axis=1)))
        return (backward.T, jnp.stack(first_cols, axis=1), jnp.stack(second_cols, axis=1))
    backward, first_sum, second_sum = lax.map(one_group, jnp.arange(group_count, dtype=jnp.int32))
    backward = jnp.transpose(backward, (1, 0, 2)).reshape(length, C)
    first_sum = first_sum.reshape(C, MODES)
    second_sum = second_sum.reshape(C, MODES)
    scaling = 1.0 / math.sqrt(TOKENS)
    grad_inputs = (backward + skip_weight[None, :] * grad_out.astype(jnp.float32)).astype(jnp.bfloat16)
    root = jnp.sqrt(rates)
    grad_residues = 0.25 * root * first_sum * scaling
    grad_log_rates = (0.125 * residues * root * first_sum - rates * weights * second_sum) * scaling
    grad_skip_weight = lax.optimization_barrier(jnp.sum(inputs.astype(jnp.float32) * grad_out.astype(jnp.float32), axis=0)) * scaling
    return (grad_inputs, grad_residues, grad_log_rates, grad_skip_weight)
```

```python
import functools
import math

import jax
import jax.numpy as jnp
import ml_dtypes
import numpy as np
from jax import lax
from jax.experimental import pallas as pl
from jax.experimental.pallas import tpu as pltpu
from jax.sharding import PartitionSpec as P

MODES = 16
BLK = 256
NODES = 24
TILE = 256
LANES = 128
GROUPS = TILE // LANES
ROWS = 8
VMEM_LIMIT = 48 * 1024 * 1024


def split_bf16(table):
    high = table.astype(ml_dtypes.bfloat16)
    low = (table - high.astype(np.float64)).astype(ml_dtypes.bfloat16)
    return high, low


@functools.cache
def tables():
    order = np.arange(NODES)
    angle = (2 * order + 1) * math.pi / (2 * NODES)
    nodes = 0.5 * BLK * (1 + np.cos(angle))
    spots = np.arange(BLK + 1.0)
    basis = ((-1.0) ** order * np.sin(angle)) / (spots[:, None] - nodes[None])
    basis = basis / basis.sum(axis=1, keepdims=True)
    ahead = basis[:BLK].T
    behind = basis[BLK - np.arange(BLK)].T
    phase = 2 * math.pi * (np.arange(BLK)[:, None] + 0.5) * np.arange(BLK)[None] / (2 * BLK)
    forward = np.concatenate([np.cos(phase), np.sin(phase)], axis=0)
    inverse = np.concatenate([np.cos(phase).T, -np.sin(phase).T], axis=1) / BLK
    bf16 = ml_dtypes.bfloat16
    trans_in = np.concatenate([forward.astype(bf16), *split_bf16(behind)], axis=0)
    trans_gr = np.concatenate([forward.astype(bf16), *split_bf16(ahead)], axis=0)
    fold = np.concatenate([ahead @ inverse, inverse[:1], np.zeros((7, 2 * BLK))], axis=0)
    fold_high, fold_low = split_bf16(fold)
    fold_table = np.concatenate([fold_high, fold_low], axis=0)
    lift_high, lift_low = split_bf16(forward @ ahead.T)
    lift_table = np.concatenate([lift_high, lift_high, lift_low], axis=1)
    spread_high, spread_low = split_bf16(behind.T)
    spread = np.concatenate([spread_high, spread_high, spread_low], axis=1)
    column = np.broadcast_to(nodes[:, None], (NODES, 128)).astype(np.float32)
    return {
        "nodes": [float(x) for x in nodes.astype(np.float32)],
        "column": column,
        "trans_in": trans_in,
        "trans_gr": trans_gr,
        "forward": forward.astype(bf16),
        "inverse": inverse.astype(bf16),
        "fold": fold_table,
        "lift": lift_table,
        "spread": spread,
    }


def dot32(left, right):
    return jnp.dot(left, right, preferred_element_type=jnp.float32)


def halves(values):
    high = values.astype(jnp.bfloat16)
    low = (values - high.astype(jnp.float32)).astype(jnp.bfloat16)
    return high, low


def sums_kernel(nodes, blocks, in_ref, gr_ref, rate_ref, tin_ref, tgr_ref, fold_ref, col_ref,
                out_ref, local_ref, uspec, gspec, mode_exp, points, cross, packed):
    log_rates = rate_ref[...].T
    rates = jnp.exp(log_rates)
    for n in range(NODES):
        mode_exp[pl.ds(n * MODES, MODES), :] = jnp.exp(rates * (-nodes[n]))
    column = col_ref[:, :1]

    def transform(b, carry):
        rows = pl.ds(pl.multiple_of(b * BLK, BLK), BLK)
        uspec[b] = dot32(tin_ref[...], in_ref[rows, :])
        gspec[b] = dot32(tgr_ref[...], gr_ref[rows, :])
        return carry

    lax.fori_loop(0, blocks, transform, 0)

    def cross_rows(j, carry):
        cos_rows = pl.ds(pl.multiple_of(j * 8, 8), 8)
        sin_rows = pl.ds(pl.multiple_of(j * 8 + BLK, 8), 8)
        real = jnp.zeros((8, TILE), jnp.float32)
        imag = jnp.zeros((8, TILE), jnp.float32)
        for b in range(blocks):
            uc, us = uspec[b, cos_rows, :], uspec[b, sin_rows, :]
            gc, gs = gspec[b, cos_rows, :], gspec[b, sin_rows, :]
            real = real + (gc * uc + gs * us)
            imag = imag + (gc * us - gs * uc)
        cross[cos_rows, :] = real
        cross[sin_rows, :] = imag
        return carry

    lax.fori_loop(0, BLK // 8, cross_rows, 0)
    high, low = halves(cross[...])
    wide = dot32(fold_ref[...], high)
    folded = wide[:32] + wide[32:] + dot32(fold_ref[:32, :], low)
    skip_row = folded[NODES:NODES + 1]

    def contract(values):
        points[0:NODES, :] = values
        points[NODES:2 * NODES, :] = values * column
        total = jnp.zeros((MODES, TILE), jnp.float32)
        moment = jnp.zeros((MODES, TILE), jnp.float32)
        for n in range(NODES):
            decay = mode_exp[pl.ds(n * MODES, MODES), :]
            total = total + decay * points[n:n + 1, :]
            moment = moment + decay * points[NODES + n:NODES + n + 1, :]
        return total, moment

    step_decay = jnp.exp(rates * (-float(BLK)))
    first, second = contract(folded[:NODES])
    zero = jnp.zeros((MODES, TILE), jnp.float32)
    top = 2 * BLK
    mid = top + NODES

    def block(b, carry):
        first, second, sum_in, mom_in, gsum, gmom, reach, offset = carry
        u_sum, u_mom = contract(uspec[b, top:mid, :] + uspec[b, mid:mid + NODES, :])
        g_sum, g_mom = contract(gspec[b, top:mid, :] + gspec[b, mid:mid + NODES, :])
        local_ref[pl.ds(pl.multiple_of(b * MODES, MODES), MODES), :] = g_sum
        first = first + g_sum * sum_in
        second = second + (g_mom * sum_in + g_sum * mom_in)
        gsum = gsum + reach * g_sum
        gmom = gmom + reach * (g_mom + offset * g_sum)
        mom_in = step_decay * (mom_in + float(BLK) * sum_in) + u_mom
        sum_in = step_decay * sum_in + u_sum
        return first, second, sum_in, mom_in, gsum, gmom, reach * step_decay, offset + float(BLK)

    first, second, sum_in, mom_in, gsum, gmom, _, _ = lax.fori_loop(
        0, blocks, block, (first, second, zero, zero, zero, zero, zero + 1.0, jnp.float32(0.0))
    )
    skip_rows = jnp.broadcast_to(skip_row, (MODES, TILE))
    parts = (first, second, sum_in, mom_in, gsum, gmom, skip_rows, rates)
    for lane in range(GROUPS):
        span = slice(lane * LANES, (lane + 1) * LANES)
        for q, part in enumerate(parts):
            packed[lane, pl.ds(q, MODES, stride=ROWS), :] = part[:, span]
        out_ref[:, span] = packed[lane]


def nearby_kernel(nodes, blocks, gr_ref, rate_ref, res_ref, skip_ref, fwd_ref, inv_ref, lift_ref,
                  near_ref, weighted_ref, impulse, filt):
    rates = jnp.exp(rate_ref[...].T)
    root = jnp.sqrt(rates)
    residues = res_ref[...].T
    weights = 0.25 * residues * root
    for n in range(NODES):
        weighted = weights * jnp.exp(rates * (-nodes[n]))
        weighted_ref[pl.ds(n * MODES, MODES), :] = weighted
        impulse[n:n + 1, :] = jnp.sum(weighted, axis=0, keepdims=True)
    high, low = halves(impulse[...])
    filt[...] = dot32(lift_ref[...], jnp.concatenate([high, low, high], axis=0))
    skip = skip_ref[...]

    def block(b, carry):
        rows = pl.ds(pl.multiple_of(b * BLK, BLK), BLK)
        grad = gr_ref[rows, :]
        spec = dot32(fwd_ref[...], grad)
        gc, gs = spec[:BLK], spec[BLK:]
        hc, hs = filt[:BLK, :], filt[BLK:, :]
        real = (gc * hc + gs * hs).astype(jnp.bfloat16)
        imag = (gc * hs - gs * hc).astype(jnp.bfloat16)
        near = dot32(inv_ref[:, :BLK], real) + dot32(inv_ref[:, BLK:], imag)
        near_ref[rows, :] = near + skip * grad.astype(jnp.float32)
        return carry

    lax.fori_loop(0, blocks, block, 0)


def scan_kernel(shards, span, in_ref, out_ref):
    decay = jnp.exp(in_ref[0, 7:8, :] * (-span))

    def row(d, q):
        return in_ref[d, q:q + 1, :]

    zero = jnp.zeros_like(decay)
    first, second, skip, sum_in, mom_in = zero, zero, zero, zero, zero
    for d in range(shards):
        gsum, gmom = row(d, 4), row(d, 5)
        first = first + (row(d, 0) + gsum * sum_in)
        second = second + (row(d, 1) + (gmom * sum_in + gsum * mom_in))
        skip = skip + row(d, 6)
        mom_in = decay * (mom_in + span * sum_in) + row(d, 3)
        sum_in = decay * sum_in + row(d, 2)
    blank = jnp.zeros((4, first.shape[1]), jnp.float32)
    back = zero
    for d in reversed(range(shards)):
        out_ref[d] = jnp.concatenate([back, first, second, skip, blank], axis=0)
        back = row(d, 4) + decay * back


def finish_kernel(blocks, scaling, near_ref, mid_ref, weighted_ref, local_ref, rate_ref, res_ref, spread_ref,
                  out_ref, gres_ref, grate_ref, gskip_ref, packed, back_scr, coef):
    rates = jnp.exp(rate_ref[...].T)
    residues = res_ref[...].T
    root = jnp.sqrt(rates)
    weights = 0.25 * residues * root
    step_decay = jnp.exp(rates * (-float(BLK)))

    for lane in range(GROUPS):
        packed[lane] = mid_ref[:, lane * LANES:(lane + 1) * LANES]

    def picked(q):
        return jnp.concatenate(
            [packed[lane, pl.ds(q, MODES, stride=ROWS), :] for lane in range(GROUPS)], axis=1
        )

    first, second = picked(1), picked(2)
    gres_ref[...] = (0.25 * root * first * scaling).T
    grate_ref[...] = ((0.125 * residues * root * first - rates * weights * second) * scaling).T
    gskip_ref[...] = mid_ref[3:4, :] * scaling
    back = picked(0)
    for b in reversed(range(blocks)):
        for lane in range(GROUPS):
            back_scr[lane, pl.ds(b, MODES, stride=blocks), :] = back[:, lane * LANES:(lane + 1) * LANES]
        back = local_ref[pl.ds(b * MODES, MODES), :] + step_decay * back
    for lane in range(GROUPS):
        span = slice(lane * LANES, (lane + 1) * LANES)
        for n in range(NODES):
            total = jnp.zeros((blocks, LANES), jnp.float32)
            for m in range(MODES):
                line = weighted_ref[n * MODES + m:n * MODES + m + 1, span]
                total = total + back_scr[lane, pl.ds(m * blocks, blocks), :] * line
            coef[lane, pl.ds(n, blocks, stride=NODES), :] = total
    for b in range(blocks):
        high, low = halves(
            jnp.concatenate([coef[lane, pl.ds(b * NODES, NODES), :] for lane in range(GROUPS)], axis=1)
        )
        far = dot32(spread_ref[...], jnp.concatenate([high, low, high], axis=0))
        rows = pl.ds(b * BLK, BLK)
        out_ref[rows, :] = (near_ref[rows, :] + far).astype(jnp.bfloat16)


def on_device(inputs, grad_out, residues, log_rates, skip_weight):
    tokens, channels = inputs.shape
    shards = lax.axis_size("ctx")
    blocks = tokens // BLK
    grid = (channels // TILE,)
    scaling = 1.0 / math.sqrt(tokens * shards)
    t = tables()
    nodes = t["nodes"]
    f32 = jnp.float32
    skip_line = skip_weight.reshape(1, channels)

    def cols(rows):
        return pl.BlockSpec((rows, TILE), lambda i: (0, i))

    per_channel = pl.BlockSpec((TILE, MODES), lambda i: (i, 0))

    def whole(table):
        return pl.BlockSpec(table.shape, lambda i: (0, 0))

    params = pltpu.CompilerParams(vmem_limit_bytes=VMEM_LIMIT)

    def cost(flops, size):
        return pl.CostEstimate(flops=int(flops), bytes_accessed=int(size), transcendentals=0)

    names = ("trans_in", "trans_gr", "fold", "column")
    consts = [jnp.asarray(t[k]) for k in names]
    spec_rows = 2 * BLK + 2 * NODES
    summed, local = pl.pallas_call(
        functools.partial(sums_kernel, nodes, blocks),
        grid=grid,
        in_specs=[cols(tokens), cols(tokens), per_channel] + [whole(c) for c in consts],
        out_specs=[cols(MODES * ROWS), cols(MODES * blocks)],
        out_shape=[
            jax.ShapeDtypeStruct((MODES * ROWS, channels), f32),
            jax.ShapeDtypeStruct((MODES * blocks, channels), f32),
        ],
        scratch_shapes=[
            pltpu.VMEM((blocks, spec_rows, TILE), f32),
            pltpu.VMEM((blocks, spec_rows, TILE), f32),
            pltpu.VMEM((NODES * MODES, TILE), f32),
            pltpu.VMEM((2 * NODES, TILE), f32),
            pltpu.VMEM((2 * BLK, TILE), f32),
            pltpu.VMEM((GROUPS, MODES * ROWS, LANES), f32),
        ],
        compiler_params=params,
        cost_estimate=cost(4 * spec_rows * tokens * channels, 8 * tokens * channels),
    )(inputs, grad_out, log_rates, *consts)

    by_mode = lax.all_to_all(
        summed.reshape(MODES, ROWS, channels), "ctx", split_axis=0, concat_axis=0, tiled=True
    )

    consts = [jnp.asarray(t[k]) for k in ("forward", "inverse", "lift")]
    nearby, weighted = pl.pallas_call(
        functools.partial(nearby_kernel, nodes, blocks),
        grid=grid,
        in_specs=[cols(tokens), per_channel, per_channel, cols(1)] + [whole(c) for c in consts],
        out_specs=[cols(tokens), cols(NODES * MODES)],
        out_shape=[
            jax.ShapeDtypeStruct((tokens, channels), f32),
            jax.ShapeDtypeStruct((NODES * MODES, channels), f32),
        ],
        scratch_shapes=[pltpu.VMEM((NODES, TILE), f32), pltpu.VMEM((2 * BLK, TILE), f32)],
        compiler_params=params,
        cost_estimate=cost(8 * BLK * tokens * channels, 6 * tokens * channels),
    )(grad_out, log_rates, residues, skip_line, *consts)

    scanned = pl.pallas_call(
        functools.partial(scan_kernel, shards, float(tokens)),
        out_shape=jax.ShapeDtypeStruct((shards, ROWS, channels), f32),
        compiler_params=params,
    )(by_mode)

    back = lax.all_to_all(scanned, "ctx", split_axis=0, concat_axis=0, tiled=True)

    spread = jnp.asarray(t["spread"])
    grad_inputs, grad_residues, grad_log_rates, grad_skip = pl.pallas_call(
        functools.partial(finish_kernel, blocks, scaling),
        grid=grid,
        in_specs=[
            cols(tokens), cols(MODES * ROWS), cols(NODES * MODES), cols(MODES * blocks),
            per_channel, per_channel, whole(spread),
        ],
        out_specs=[cols(tokens), per_channel, per_channel, cols(1)],
        out_shape=[
            jax.ShapeDtypeStruct((tokens, channels), jnp.bfloat16),
            jax.ShapeDtypeStruct((channels, MODES), f32),
            jax.ShapeDtypeStruct((channels, MODES), f32),
            jax.ShapeDtypeStruct((1, channels), f32),
        ],
        scratch_shapes=[
            pltpu.VMEM((GROUPS, MODES * ROWS, LANES), f32),
            pltpu.VMEM((GROUPS, MODES * blocks, LANES), f32),
            pltpu.VMEM((GROUPS, NODES * blocks, LANES), f32),
        ],
        compiler_params=params,
    )(nearby, back.reshape(MODES * ROWS, channels), weighted, local, log_rates, residues, spread)
    return grad_inputs, grad_residues, grad_log_rates, grad_skip.reshape(channels)


def solution(mesh):
    placed = (P("ctx", "ch"), P("ctx", "ch"), P("ch", None), P("ch", None), P("ch"))
    return jax.shard_map(
        on_device,
        mesh=mesh,
        in_specs=placed,
        out_specs=(P("ctx", "ch"), P("ch", None), P("ch", None), P("ch")),
        check_vma=False,
    )
```

```python
import functools
import math

import jax
import jax.numpy as jnp
import ml_dtypes
import numpy as np
from jax import lax
from jax.experimental import pallas as pl
from jax.experimental.pallas import tpu as pltpu
from jax.sharding import PartitionSpec as P

MODES = 16
BLK = 256
NODES = 24
TILE = 256
LANES = 128
GROUPS = TILE // LANES
ROWS = 8
PAIRS = 4
VMEM_LIMIT = 24 * 1024 * 1024


def split_bf16(table):
    high = table.astype(ml_dtypes.bfloat16)
    low = (table - high.astype(np.float64)).astype(ml_dtypes.bfloat16)
    return high, low


@functools.cache
def tables():
    order = np.arange(NODES)
    angle = (2 * order + 1) * math.pi / (2 * NODES)
    nodes = 0.5 * BLK * (1 + np.cos(angle))
    spots = np.arange(BLK + 1.0)
    basis = ((-1.0) ** order * np.sin(angle)) / (spots[:, None] - nodes[None])
    basis = basis / basis.sum(axis=1, keepdims=True)
    ahead = basis[:BLK].T
    behind = basis[BLK - np.arange(BLK)].T
    phase = 2 * math.pi * (np.arange(BLK)[:, None] + 0.5) * np.arange(BLK)[None] / (2 * BLK)
    forward = np.concatenate([np.cos(phase), np.sin(phase)], axis=0)
    inverse = np.concatenate([np.cos(phase).T, -np.sin(phase).T], axis=1) / BLK
    bf16 = ml_dtypes.bfloat16
    trans_in = np.concatenate([forward.astype(bf16), *split_bf16(behind)], axis=0)
    trans_gr = np.concatenate([forward.astype(bf16), *split_bf16(ahead)], axis=0)
    fold = np.concatenate([ahead @ inverse, inverse[:1], np.zeros((7, 2 * BLK))], axis=0)
    fold_high, fold_low = split_bf16(fold)
    fold_table = np.concatenate([fold_high, fold_low], axis=0)
    lift_high, lift_low = split_bf16(forward @ ahead.T)
    lift_table = np.concatenate([lift_high, lift_high, lift_low], axis=1)
    spread_high, spread_low = split_bf16(behind.T)
    spread = np.concatenate([spread_high, spread_high, spread_low], axis=1)
    return {
        "nodes": [float(x) for x in nodes.astype(np.float32)],
        "trans_in": trans_in,
        "trans_gr": trans_gr,
        "forward": forward.astype(bf16),
        "inverse": inverse.astype(bf16),
        "fold": fold_table,
        "lift": lift_table,
        "spread": spread,
    }


def dot32(left, right):
    return jnp.dot(left, right, preferred_element_type=jnp.float32)


def halves(values):
    high = values.astype(jnp.bfloat16)
    low = (values - high.astype(jnp.float32)).astype(jnp.bfloat16)
    return high, low


def sums_kernel(nodes, blocks, in_hbm, gr_hbm, rate_hbm, tin_hbm, tgr_hbm, fold_hbm,
                out_ref, local_ref, rate_ref, in_ref, gr_ref, tin_ref, tgr_ref, fold_ref, uspec, gspec,
                mode_exp, points, cross, packed, table_sem, in_sem, gr_sem):
    channels = rate_ref.shape[1]
    tiles = channels // TILE
    spec_rows = 2 * BLK + 2 * NODES

    def tables_in():
        return [
            pltpu.make_async_copy(src, dst, table_sem.at[k])
            for k, (src, dst) in enumerate(((tin_hbm, tin_ref), (tgr_hbm, tgr_ref), (fold_hbm, fold_ref)))
        ]

    def block_in(b):
        rows = pl.ds(b * BLK, BLK)
        return (
            pltpu.make_async_copy(in_hbm.at[rows, :], in_ref.at[rows, :], in_sem.at[b]),
            pltpu.make_async_copy(gr_hbm.at[rows, :], gr_ref.at[rows, :], gr_sem.at[b]),
        )

    rate_copy = pltpu.make_async_copy(rate_hbm, rate_ref, table_sem.at[3])
    rate_copy.start()
    table_copies = tables_in()
    table_copies[0].start()
    block_copies = [block_in(b) for b in range(blocks)]
    block_copies[0][0].start()
    table_copies[1].start()
    block_copies[0][1].start()
    for b in range(1, blocks):
        block_copies[b][0].start()
        block_copies[b][1].start()
    table_copies[2].start()

    rate_copy.wait()
    rates = jnp.exp(rate_ref[...])
    step_decay = jnp.exp(rates * (-float(BLK)))
    for n in range(NODES):
        mode_exp[pl.ds(n * MODES, MODES), :] = jnp.exp(rates * (-nodes[n]))

    def lanes(c):
        return slice(c * TILE, (c + 1) * TILE)

    def transform(b):
        slot = b % PAIRS
        rows = slice(b * BLK, (b + 1) * BLK)

        def product(spec, table, data, c):
            def emit():
                spec[slot, :, lanes(c)] = dot32(table[...], data[rows, lanes(c)])

            return emit

        return [
            product(spec, table, data, c)
            for c in range(tiles)
            for spec, table, data in ((uspec, tin_ref, in_ref), (gspec, tgr_ref, gr_ref))
        ]

    def cross_rows(first_block, c, low, high):
        def emit():
            for j in range(low, high):
                cos_rows = slice(j * 8, j * 8 + 8)
                sin_rows = slice(BLK + j * 8, BLK + j * 8 + 8)
                real, imag = None, None
                for b in (first_block, first_block + 1):
                    slot = b % PAIRS
                    uc, us = uspec[slot, cos_rows, lanes(c)], uspec[slot, sin_rows, lanes(c)]
                    gc, gs = gspec[slot, cos_rows, lanes(c)], gspec[slot, sin_rows, lanes(c)]
                    re, im = gc * uc + gs * us, gc * us - gs * uc
                    real = re if real is None else real + re
                    imag = im if imag is None else imag + im
                if first_block:
                    real = real + cross[cos_rows, lanes(c)]
                    imag = imag + cross[sin_rows, lanes(c)]
                cross[cos_rows, lanes(c)] = real
                cross[sin_rows, lanes(c)] = imag

        return emit

    def contract(c, series):
        count = len(series)
        for k, values in enumerate(series):
            points[c, k] = values
        zero = jnp.zeros((MODES, TILE), jnp.float32)
        totals, moments = [zero] * count, [zero] * count
        for n in range(NODES):
            decay = mode_exp[n * MODES:(n + 1) * MODES, lanes(c)]
            scaled = decay * nodes[n]
            for k in range(count):
                line = points[c, k, n:n + 1, :]
                totals[k] = totals[k] + decay * line
                moments[k] = moments[k] + scaled * line
        return totals, moments

    top = 2 * BLK
    mid = top + NODES
    zero = jnp.zeros((MODES, TILE), jnp.float32)
    state = [[zero, zero, zero, zero, zero, zero, zero + 1.0] for _ in range(tiles)]

    def modal_pair(first_block, c):
        def emit():
            first, second, sum_in, mom_in, gsum, gmom, reach = state[c]
            series = []
            for b in (first_block, first_block + 1):
                for spec in (uspec, gspec):
                    slot = b % PAIRS
                    series.append(spec[slot, top:mid, lanes(c)] + spec[slot, mid:spec_rows, lanes(c)])
            totals, moments = contract(c, series)
            decay = step_decay[:, lanes(c)]
            for k in range(2):
                b = first_block + k
                u_sum, g_sum = totals[2 * k], totals[2 * k + 1]
                u_mom, g_mom = moments[2 * k], moments[2 * k + 1]
                local_ref[b * MODES:(b + 1) * MODES, lanes(c)] = g_sum
                first = first + g_sum * sum_in
                second = second + (g_mom * sum_in + g_sum * mom_in)
                gsum = gsum + reach * g_sum
                gmom = gmom + reach * (g_mom + float(BLK * b) * g_sum)
                mom_in = decay * (mom_in + float(BLK) * sum_in) + u_mom
                sum_in = decay * sum_in + u_sum
                reach = reach * decay
            state[c] = [first, second, sum_in, mom_in, gsum, gmom, reach]

        return emit

    table_copies[0].wait()
    table_copies[1].wait()
    def pair_work(first_block):
        work = []
        for c in range(tiles):
            work.append(cross_rows(first_block, c, 0, BLK // 16))
            work.append(modal_pair(first_block, c))
            work.append(cross_rows(first_block, c, BLK // 16, BLK // 8))
        return work

    for pair in range(0, blocks, 2):
        for b in (pair, pair + 1):
            for copy in block_copies[b]:
                copy.wait()
        products = transform(pair) + transform(pair + 1)
        work = pair_work(pair - 2) if pair else []
        for k, product in enumerate(products):
            product()
            if k < len(work):
                work[k]()
    for emit in pair_work(blocks - 2):
        emit()
    table_copies[2].wait()
    for c in range(tiles):
        high, low = halves(cross[:, lanes(c)])
        wide = dot32(fold_ref[...], high)
        folded = wide[:32] + wide[32:] + dot32(fold_ref[:32, :], low)
        totals, moments = contract(c, [folded[:NODES]])
        first, second, sum_in, mom_in, gsum, gmom, _ = state[c]
        skip_rows = jnp.broadcast_to(folded[NODES:NODES + 1], (MODES, TILE))
        parts = (first + totals[0], second + moments[0], sum_in, mom_in, gsum, gmom, skip_rows, rates[:, lanes(c)])
        for half in range(GROUPS):
            span = slice(half * LANES, (half + 1) * LANES)
            group = c * GROUPS + half
            for q, part in enumerate(parts):
                packed[group, pl.ds(q, MODES, stride=ROWS), :] = part[:, span]
            out_ref[:, group * LANES:(group + 1) * LANES] = packed[group]


def nearby_kernel(nodes, blocks, gr_ref, rate_ref, res_ref, skip_ref, fwd_ref, inv_ref, lift_ref,
                  near_ref, weighted_ref, impulse, filt):
    rates = jnp.exp(rate_ref[...])
    root = jnp.sqrt(rates)
    residues = res_ref[...]
    weights = 0.25 * residues * root
    for n in range(NODES):
        weighted = weights * jnp.exp(rates * (-nodes[n]))
        weighted_ref[pl.ds(n * MODES, MODES), :] = weighted
        impulse[n:n + 1, :] = jnp.sum(weighted, axis=0, keepdims=True)
    high, low = halves(impulse[...])
    filt[...] = dot32(lift_ref[...], jnp.concatenate([high, low, high], axis=0))
    skip = skip_ref[...]

    for b in range(blocks):
        rows = slice(b * BLK, (b + 1) * BLK)
        grad = gr_ref[rows, :]
        spec = dot32(fwd_ref[...], grad)
        gc, gs = spec[:BLK], spec[BLK:]
        hc, hs = filt[:BLK, :], filt[BLK:, :]
        real = (gc * hc + gs * hs).astype(jnp.bfloat16)
        imag = (gc * hs - gs * hc).astype(jnp.bfloat16)
        near = dot32(inv_ref[:, :BLK], real) + dot32(inv_ref[:, BLK:], imag)
        near_ref[rows, :] = near + skip * grad.astype(jnp.float32)


def scan_kernel(shards, span, in_ref, out_ref):
    decay = jnp.exp(in_ref[0, 7:8, :] * (-span))

    def row(d, q):
        return in_ref[d, q:q + 1, :]

    zero = jnp.zeros_like(decay)
    first, second, skip, sum_in, mom_in = zero, zero, zero, zero, zero
    for d in range(shards):
        gsum, gmom = row(d, 4), row(d, 5)
        first = first + (row(d, 0) + gsum * sum_in)
        second = second + (row(d, 1) + (gmom * sum_in + gsum * mom_in))
        skip = skip + row(d, 6)
        mom_in = decay * (mom_in + span * sum_in) + row(d, 3)
        sum_in = decay * sum_in + row(d, 2)
    blank = jnp.zeros((4, first.shape[1]), jnp.float32)
    back = zero
    for d in reversed(range(shards)):
        out_ref[d] = jnp.concatenate([back, first, second, skip, blank], axis=0)
        back = row(d, 4) + decay * back


def finish_kernel(blocks, scaling, near_hbm, mid_ref, weighted_ref, local_ref, rate_ref, res_ref, spread_ref,
                  out_hbm, gres_ref, grate_ref, gskip_ref, near_ref, out_ref, packed, back_scr, coef,
                  near_sem, out_sem):
    channels = rate_ref.shape[1]
    groups = channels // LANES

    def near_in(b):
        rows = pl.ds(b * BLK, BLK)
        return pltpu.make_async_copy(near_hbm.at[rows, :], near_ref.at[rows, :], near_sem.at[b])

    def block_out(b):
        rows = pl.ds(b * BLK, BLK)
        return pltpu.make_async_copy(out_ref.at[rows, :], out_hbm.at[rows, :], out_sem.at[b])

    for b in range(blocks):
        near_in(b).start()

    rates = jnp.exp(rate_ref[...])
    residues = res_ref[...]
    root = jnp.sqrt(rates)
    weights = 0.25 * residues * root
    step_decay = jnp.exp(rates * (-float(BLK)))
    for lane in range(groups):
        packed[lane] = mid_ref[:, lane * LANES:(lane + 1) * LANES]

    def picked(q):
        return jnp.concatenate(
            [packed[lane, pl.ds(q, MODES, stride=ROWS), :] for lane in range(groups)], axis=1
        )

    back = picked(0)
    for b in reversed(range(blocks)):
        for lane in range(groups):
            back_scr[lane, pl.ds(b, MODES, stride=blocks), :] = back[:, lane * LANES:(lane + 1) * LANES]
        back = local_ref[b * MODES:(b + 1) * MODES, :] + step_decay * back
    for lane in range(groups):
        span = slice(lane * LANES, (lane + 1) * LANES)
        for n in range(NODES):
            total = jnp.zeros((blocks, LANES), jnp.float32)
            for m in range(MODES):
                line = weighted_ref[n * MODES + m:n * MODES + m + 1, span]
                total = total + back_scr[lane, m * blocks:(m + 1) * blocks, :] * line
            coef[lane, pl.ds(n, blocks, stride=NODES), :] = total
    for b in range(blocks):
        high, low = halves(
            jnp.concatenate([coef[lane, b * NODES:(b + 1) * NODES, :] for lane in range(groups)], axis=1)
        )
        far = dot32(spread_ref[...], jnp.concatenate([high, low, high], axis=0))
        rows = slice(b * BLK, (b + 1) * BLK)
        near_in(b).wait()
        out_ref[rows, :] = (near_ref[rows, :] + far).astype(jnp.bfloat16)
        block_out(b).start()
    first, second = picked(1), picked(2)
    gres_ref[...] = 0.25 * root * first * scaling
    grate_ref[...] = (0.125 * residues * root * first - rates * weights * second) * scaling
    gskip_ref[...] = mid_ref[3:4, :] * scaling
    for b in range(blocks):
        block_out(b).wait()


def cols(rows):
    return pl.BlockSpec((rows, TILE), lambda i: (0, i))


def whole(table):
    return pl.BlockSpec(table.shape, lambda i: (0, 0))


def f32_rows(rows, channels):
    return jax.ShapeDtypeStruct((rows, channels), jnp.float32)


def cost(flops, size):
    return pl.CostEstimate(flops=int(flops), bytes_accessed=int(size), transcendentals=0)


PARAMS = pltpu.CompilerParams(vmem_limit_bytes=VMEM_LIMIT)


def call_sums(inputs, grad_out, log_rates):
    tokens, channels = inputs.shape
    blocks = tokens // BLK
    t = tables()
    consts = [jnp.asarray(t[k]) for k in ("trans_in", "trans_gr", "fold")]
    spec_rows = 2 * BLK + 2 * NODES
    far = pl.BlockSpec(memory_space=pltpu.HBM)
    near = pl.BlockSpec(memory_space=pltpu.VMEM)
    return pl.pallas_call(
        functools.partial(sums_kernel, t["nodes"], blocks),
        in_specs=[far] * 6,
        out_specs=[near, near],
        out_shape=[f32_rows(MODES * ROWS, channels), f32_rows(MODES * blocks, channels)],
        scratch_shapes=[
            pltpu.VMEM((MODES, channels), jnp.float32),
            pltpu.VMEM((tokens, channels), jnp.bfloat16),
            pltpu.VMEM((tokens, channels), jnp.bfloat16),
            pltpu.VMEM(consts[0].shape, jnp.bfloat16),
            pltpu.VMEM(consts[1].shape, jnp.bfloat16),
            pltpu.VMEM(consts[2].shape, jnp.bfloat16),
            pltpu.VMEM((PAIRS, spec_rows, channels), jnp.float32),
            pltpu.VMEM((PAIRS, spec_rows, channels), jnp.float32),
            pltpu.VMEM((NODES * MODES, channels), jnp.float32),
            pltpu.VMEM((channels // TILE, 4, NODES, TILE), jnp.float32),
            pltpu.VMEM((2 * BLK, channels), jnp.float32),
            pltpu.VMEM((channels // LANES, MODES * ROWS, LANES), jnp.float32),
            pltpu.SemaphoreType.DMA((4,)),
            pltpu.SemaphoreType.DMA((blocks,)),
            pltpu.SemaphoreType.DMA((blocks,)),
        ],
        compiler_params=PARAMS,
        cost_estimate=cost(4 * spec_rows * tokens * channels, 8 * tokens * channels),
    )(*(pltpu.with_memory_space_constraint(x, pltpu.HBM) for x in (inputs, grad_out, log_rates, *consts)))


def call_nearby(grad_out, log_rates, residues, skip_line):
    tokens, channels = grad_out.shape
    t = tables()
    consts = [jnp.asarray(t[k]) for k in ("forward", "inverse", "lift")]
    return pl.pallas_call(
        functools.partial(nearby_kernel, t["nodes"], tokens // BLK),
        grid=(channels // TILE,),
        in_specs=[cols(tokens), cols(MODES), cols(MODES), cols(1)] + [whole(c) for c in consts],
        out_specs=[cols(tokens), cols(NODES * MODES)],
        out_shape=[f32_rows(tokens, channels), f32_rows(NODES * MODES, channels)],
        scratch_shapes=[pltpu.VMEM((NODES, TILE), jnp.float32), pltpu.VMEM((2 * BLK, TILE), jnp.float32)],
        compiler_params=PARAMS,
        cost_estimate=cost(8 * BLK * tokens * channels, 6 * tokens * channels),
    )(grad_out, log_rates, residues, skip_line, *consts)


def call_scan(by_mode, tokens):
    return pl.pallas_call(
        functools.partial(scan_kernel, by_mode.shape[0], float(tokens)),
        out_shape=jax.ShapeDtypeStruct(by_mode.shape, jnp.float32),
        compiler_params=PARAMS,
    )(by_mode)


def call_finish(scaling, nearby, back, weighted, local, log_rates, residues):
    tokens, channels = nearby.shape
    blocks = tokens // BLK
    spread = jnp.asarray(tables()["spread"])
    far = pl.BlockSpec(memory_space=pltpu.HBM)
    near = pl.BlockSpec(memory_space=pltpu.VMEM)
    return pl.pallas_call(
        functools.partial(finish_kernel, blocks, scaling),
        in_specs=[far] + [near] * 6,
        out_specs=[far, near, near, near],
        out_shape=[
            jax.ShapeDtypeStruct((tokens, channels), jnp.bfloat16),
            f32_rows(MODES, channels),
            f32_rows(MODES, channels),
            f32_rows(1, channels),
        ],
        scratch_shapes=[
            pltpu.VMEM((tokens, channels), nearby.dtype),
            pltpu.VMEM((tokens, channels), jnp.bfloat16),
            pltpu.VMEM((channels // LANES, MODES * ROWS, LANES), jnp.float32),
            pltpu.VMEM((channels // LANES, MODES * blocks, LANES), jnp.float32),
            pltpu.VMEM((channels // LANES, NODES * blocks, LANES), jnp.float32),
            pltpu.SemaphoreType.DMA((blocks,)),
            pltpu.SemaphoreType.DMA((blocks,)),
        ],
        compiler_params=PARAMS,
    )(pltpu.with_memory_space_constraint(nearby, pltpu.HBM), back, weighted, local, log_rates, residues, spread)


def on_device(inputs, grad_out, residues, log_rates, skip_weight):
    tokens, channels = inputs.shape
    scaling = 1.0 / math.sqrt(tokens * lax.axis_size("ctx"))
    residues, log_rates = residues.T, log_rates.T
    summed, local = call_sums(inputs, grad_out, log_rates)
    by_mode = lax.all_to_all(
        summed.reshape(MODES, ROWS, channels), "ctx", split_axis=0, concat_axis=0, tiled=True
    )
    nearby, weighted = call_nearby(grad_out, log_rates, residues, skip_weight.reshape(1, channels))
    scanned = call_scan(by_mode, tokens)
    back = lax.all_to_all(scanned, "ctx", split_axis=0, concat_axis=0, tiled=True)
    grad_inputs, grad_residues, grad_log_rates, grad_skip = call_finish(
        scaling, nearby, back.reshape(MODES * ROWS, channels), weighted, local, log_rates, residues
    )
    return grad_inputs, grad_residues.T, grad_log_rates.T, grad_skip.reshape(channels)


def solution(mesh):
    placed = (P("ctx", "ch"), P("ctx", "ch"), P("ch", None), P("ch", None), P("ch"))
    return jax.shard_map(
        on_device,
        mesh=mesh,
        in_specs=placed,
        out_specs=(P("ctx", "ch"), P("ch", None), P("ch", None), P("ch")),
        check_vma=False,
    )
```

```python
import functools
import math

import jax
import jax.numpy as jnp
import ml_dtypes
import numpy as np
from jax import lax
from jax.experimental import pallas as pl
from jax.experimental.pallas import tpu as pltpu
from jax.sharding import PartitionSpec as P

MODES = 16
BLK = 256
NODES = 24
TILE = 256
LANES = 128
GROUPS = TILE // LANES
ROWS = 8
PAIRS = 4
SCHEDULE = ((0, 1), (2, 3), (4, 5), (6,), (7,))
NEAR_TYPE = jnp.bfloat16
VMEM_LIMIT = 24 * 1024 * 1024


def split_bf16(table):
    high = table.astype(ml_dtypes.bfloat16)
    low = (table - high.astype(np.float64)).astype(ml_dtypes.bfloat16)
    return high, low


@functools.cache
def tables():
    order = np.arange(NODES)
    angle = (2 * order + 1) * math.pi / (2 * NODES)
    nodes = 0.5 * BLK * (1 + np.cos(angle))
    spots = np.arange(BLK + 1.0)
    basis = ((-1.0) ** order * np.sin(angle)) / (spots[:, None] - nodes[None])
    basis = basis / basis.sum(axis=1, keepdims=True)
    ahead = basis[:BLK].T
    behind = basis[BLK - np.arange(BLK)].T
    phase = 2 * math.pi * (np.arange(BLK)[:, None] + 0.5) * np.arange(BLK)[None] / (2 * BLK)
    forward = np.concatenate([np.cos(phase), np.sin(phase)], axis=0)
    inverse = np.concatenate([np.cos(phase).T, -np.sin(phase).T], axis=1) / BLK
    bf16 = ml_dtypes.bfloat16
    trans_in = np.concatenate([forward.astype(bf16), *split_bf16(behind)], axis=0)
    trans_gr = np.concatenate([forward.astype(bf16), *split_bf16(ahead)], axis=0)
    fold = np.concatenate([ahead @ inverse, inverse[:1], np.zeros((7, 2 * BLK))], axis=0)
    fold_high, fold_low = split_bf16(fold)
    fold_table = np.concatenate([fold_high, fold_low], axis=0)
    lift_high, lift_low = split_bf16(forward @ ahead.T)
    lift_table = np.concatenate([lift_high, lift_high, lift_low], axis=1)
    spread_high, spread_low = split_bf16(behind.T)
    spread = np.concatenate([spread_high, spread_high, spread_low], axis=1)
    return {
        "nodes": [float(x) for x in nodes.astype(np.float32)],
        "trans_in": trans_in,
        "trans_gr": trans_gr,
        "forward": forward.astype(bf16),
        "inverse": inverse.astype(bf16),
        "fold": fold_table,
        "lift": lift_table,
        "spread": spread,
    }


def dot32(left, right):
    return jnp.dot(left, right, preferred_element_type=jnp.float32)


def halves(values):
    high = values.astype(jnp.bfloat16)
    low = (values - high.astype(jnp.float32)).astype(jnp.bfloat16)
    return high, low


def sums_kernel(nodes, blocks, in_hbm, gr_hbm, rate_hbm, tin_hbm, tgr_hbm, fold_hbm,
                out_ref, local_ref, rate_ref, in_ref, gr_ref, tin_ref, tgr_ref, fold_ref, uspec, gspec,
                mode_exp, points, cross, packed, table_sem, in_sem, gr_sem):
    channels = rate_ref.shape[1]
    tiles = channels // TILE
    spec_rows = 2 * BLK + 2 * NODES

    def tables_in():
        return [
            pltpu.make_async_copy(src, dst, table_sem.at[k])
            for k, (src, dst) in enumerate(((tin_hbm, tin_ref), (tgr_hbm, tgr_ref), (fold_hbm, fold_ref)))
        ]

    def block_in(b):
        rows = pl.ds(b * BLK, BLK)
        return (
            pltpu.make_async_copy(in_hbm.at[rows, :], in_ref.at[rows, :], in_sem.at[b]),
            pltpu.make_async_copy(gr_hbm.at[rows, :], gr_ref.at[rows, :], gr_sem.at[b]),
        )

    rate_copy = pltpu.make_async_copy(rate_hbm, rate_ref, table_sem.at[3])
    rate_copy.start()
    table_copies = tables_in()
    table_copies[0].start()
    block_copies = [block_in(b) for b in range(blocks)]
    block_copies[0][0].start()
    table_copies[1].start()
    block_copies[0][1].start()
    for b in range(1, blocks):
        block_copies[b][0].start()
        block_copies[b][1].start()
    table_copies[2].start()

    rate_copy.wait()
    rates = jnp.exp(rate_ref[...])
    step_decay = jnp.exp(rates * (-float(BLK)))
    for n in range(NODES):
        mode_exp[pl.ds(n * MODES, MODES), :] = jnp.exp(rates * (-nodes[n]))

    def lanes(c):
        return slice(c * TILE, (c + 1) * TILE)

    def transform(b):
        slot = b % PAIRS
        rows = slice(b * BLK, (b + 1) * BLK)

        def product(spec, table, data, c):
            def emit():
                spec[slot, :, lanes(c)] = dot32(table[...], data[rows, lanes(c)])

            return emit

        return [
            product(spec, table, data, c)
            for c in range(tiles)
            for spec, table, data in ((uspec, tin_ref, in_ref), (gspec, tgr_ref, gr_ref))
        ]

    def cross_rows(group, c, low, high):
        def emit():
            for j in range(low, high):
                cos_rows = slice(j * 8, j * 8 + 8)
                sin_rows = slice(BLK + j * 8, BLK + j * 8 + 8)
                real, imag = None, None
                for b in group:
                    slot = b % PAIRS
                    uc, us = uspec[slot, cos_rows, lanes(c)], uspec[slot, sin_rows, lanes(c)]
                    gc, gs = gspec[slot, cos_rows, lanes(c)], gspec[slot, sin_rows, lanes(c)]
                    re, im = gc * uc + gs * us, gc * us - gs * uc
                    real = re if real is None else real + re
                    imag = im if imag is None else imag + im
                if group[0]:
                    real = real + cross[cos_rows, lanes(c)]
                    imag = imag + cross[sin_rows, lanes(c)]
                cross[cos_rows, lanes(c)] = real
                cross[sin_rows, lanes(c)] = imag

        return emit

    def contract(c, series):
        count = len(series)
        for k, values in enumerate(series):
            points[c, k] = values
        zero = jnp.zeros((MODES, TILE), jnp.float32)
        totals, moments = [zero] * count, [zero] * count
        for n in range(NODES):
            decay = mode_exp[n * MODES:(n + 1) * MODES, lanes(c)]
            scaled = decay * nodes[n]
            for k in range(count):
                line = points[c, k, n:n + 1, :]
                totals[k] = totals[k] + decay * line
                moments[k] = moments[k] + scaled * line
        return totals, moments

    top = 2 * BLK
    mid = top + NODES
    zero = jnp.zeros((MODES, TILE), jnp.float32)
    state = [[zero, zero, zero, zero, zero, zero, zero + 1.0] for _ in range(tiles)]

    def modal(group, c):
        def emit():
            first, second, sum_in, mom_in, gsum, gmom, reach = state[c]
            series = []
            for b in group:
                for spec in (uspec, gspec):
                    slot = b % PAIRS
                    series.append(spec[slot, top:mid, lanes(c)] + spec[slot, mid:spec_rows, lanes(c)])
            totals, moments = contract(c, series)
            decay = step_decay[:, lanes(c)]
            for k, b in enumerate(group):
                u_sum, g_sum = totals[2 * k], totals[2 * k + 1]
                u_mom, g_mom = moments[2 * k], moments[2 * k + 1]
                local_ref[b * MODES:(b + 1) * MODES, lanes(c)] = g_sum
                first = first + g_sum * sum_in
                second = second + (g_mom * sum_in + g_sum * mom_in)
                gsum = gsum + reach * g_sum
                gmom = gmom + reach * (g_mom + float(BLK * b) * g_sum)
                mom_in = decay * (mom_in + float(BLK) * sum_in) + u_mom
                sum_in = decay * sum_in + u_sum
                reach = reach * decay
            state[c] = [first, second, sum_in, mom_in, gsum, gmom, reach]

        return emit

    table_copies[0].wait()
    table_copies[1].wait()
    def vector_work(group):
        work = []
        for c in range(tiles):
            work.append(cross_rows(group, c, 0, BLK // 16))
            work.append(modal(group, c))
            work.append(cross_rows(group, c, BLK // 16, BLK // 8))
        return work

    groups = SCHEDULE
    work = []
    for group in groups:
        products = []
        for b in group:
            for copy in block_copies[b]:
                copy.wait()
            products += transform(b)
        done = 0
        for k, product in enumerate(products):
            upto = (k + 1) * len(work) // len(products)
            for emit in work[done:upto]:
                emit()
            done = upto
            product()
        work = vector_work(group)
    for emit in work:
        emit()
    table_copies[2].wait()
    for c in range(tiles):
        high, low = halves(cross[:, lanes(c)])
        wide = dot32(fold_ref[...], high)
        folded = wide[:32] + wide[32:] + dot32(fold_ref[:32, :], low)
        totals, moments = contract(c, [folded[:NODES]])
        first, second, sum_in, mom_in, gsum, gmom, _ = state[c]
        skip_rows = jnp.broadcast_to(folded[NODES:NODES + 1], (MODES, TILE))
        parts = (first + totals[0], second + moments[0], sum_in, mom_in, gsum, gmom, skip_rows, rates[:, lanes(c)])
        for half in range(GROUPS):
            span = slice(half * LANES, (half + 1) * LANES)
            group = c * GROUPS + half
            for q, part in enumerate(parts):
                packed[group, pl.ds(q, MODES, stride=ROWS), :] = part[:, span]
            out_ref[:, group * LANES:(group + 1) * LANES] = packed[group]


def nearby_kernel(nodes, blocks, gr_hbm, rate_ref, res_ref, skip_ref, fwd_hbm, inv_hbm, lift_hbm,
                  near_ref, weighted_ref, gr_ref, fwd_ref, inv_ref, lift_ref, impulse, filt, response,
                  table_sem, gr_sem):
    channels = rate_ref.shape[1]
    tiles = channels // TILE

    def table_in(k):
        src, dst = ((lift_hbm, lift_ref), (fwd_hbm, fwd_ref), (inv_hbm, inv_ref))[k]
        return pltpu.make_async_copy(src, dst, table_sem.at[k])

    def block_in(b):
        rows = pl.ds(b * BLK, BLK)
        return pltpu.make_async_copy(gr_hbm.at[rows, :], gr_ref.at[rows, :], gr_sem.at[b])

    for k in range(3):
        table_in(k).start()
    for b in range(blocks):
        block_in(b).start()

    rates = jnp.exp(rate_ref[...])
    weights = 0.25 * res_ref[...] * jnp.sqrt(rates)
    for n in range(NODES):
        weighted = weights * jnp.exp(rates * (-nodes[n]))
        weighted_ref[n * MODES:(n + 1) * MODES, :] = weighted
        impulse[n:n + 1, :] = jnp.sum(weighted, axis=0, keepdims=True)
    high, low = halves(impulse[...])
    table_in(0).wait()
    filt[...] = dot32(lift_ref[...], jnp.concatenate([high, low, high], axis=0))
    skip = skip_ref[...]
    table_in(1).wait()
    table_in(2).wait()
    for b in range(blocks):
        block_in(b).wait()
        rows = slice(b * BLK, (b + 1) * BLK)
        slot = b % 2
        for c in range(tiles):
            lanes = slice(c * TILE, (c + 1) * TILE)
            spec = dot32(fwd_ref[...], gr_ref[rows, lanes])
            gc, gs = spec[:BLK], spec[BLK:]
            hc, hs = filt[:BLK, lanes], filt[BLK:, lanes]
            response[slot, :BLK, lanes] = (gc * hc + gs * hs).astype(jnp.bfloat16)
            response[slot, BLK:, lanes] = (gc * hs - gs * hc).astype(jnp.bfloat16)
        for c in range(tiles):
            lanes = slice(c * TILE, (c + 1) * TILE)
            near = dot32(inv_ref[...], response[slot, :, lanes])
            near = near + skip[:, lanes] * gr_ref[rows, lanes].astype(jnp.float32)
            near_ref[rows, lanes] = near.astype(NEAR_TYPE)


def scan_kernel(shards, span, in_ref, out_ref):
    decay = jnp.exp(in_ref[0, 7:8, :] * (-span))

    def row(d, q):
        return in_ref[d, q:q + 1, :]

    zero = jnp.zeros_like(decay)
    first, second, skip, sum_in, mom_in = zero, zero, zero, zero, zero
    for d in range(shards):
        gsum, gmom = row(d, 4), row(d, 5)
        first = first + (row(d, 0) + gsum * sum_in)
        second = second + (row(d, 1) + (gmom * sum_in + gsum * mom_in))
        skip = skip + row(d, 6)
        mom_in = decay * (mom_in + span * sum_in) + row(d, 3)
        sum_in = decay * sum_in + row(d, 2)
    blank = jnp.zeros((4, first.shape[1]), jnp.float32)
    back = zero
    for d in reversed(range(shards)):
        out_ref[d] = jnp.concatenate([back, first, second, skip, blank], axis=0)
        back = row(d, 4) + decay * back


def finish_kernel(blocks, scaling, near_ref, mid_ref, weighted_ref, local_ref, rate_ref, res_ref, spread_ref,
                  out_hbm, gres_hbm, grate_hbm, gskip_hbm, out_ref, gres_ref, grate_ref, gskip_ref,
                  packed, back_scr, coef, out_sem, grad_sem):
    channels = rate_ref.shape[1]
    groups = channels // LANES

    def block_out(b):
        rows = pl.ds(b * BLK, BLK)
        return pltpu.make_async_copy(out_ref.at[rows, :], out_hbm.at[rows, :], out_sem.at[b])

    rates = jnp.exp(rate_ref[...])
    residues = res_ref[...]
    root = jnp.sqrt(rates)
    weights = 0.25 * residues * root
    step_decay = jnp.exp(rates * (-float(BLK)))
    for lane in range(groups):
        packed[lane] = mid_ref[:, lane * LANES:(lane + 1) * LANES]

    def picked(q):
        return jnp.concatenate(
            [packed[lane, pl.ds(q, MODES, stride=ROWS), :] for lane in range(groups)], axis=1
        )

    first, second = picked(1), picked(2)
    gres_ref[...] = 0.25 * root * first * scaling
    grate_ref[...] = (0.125 * residues * root * first - rates * weights * second) * scaling
    gskip_ref[...] = mid_ref[3:4, :] * scaling
    grad_copies = [
        pltpu.make_async_copy(src, dst, grad_sem.at[k])
        for k, (src, dst) in enumerate(((gres_ref, gres_hbm), (grate_ref, grate_hbm), (gskip_ref, gskip_hbm)))
    ]
    for copy in grad_copies:
        copy.start()

    back = picked(0)
    for b in reversed(range(blocks)):
        for lane in range(groups):
            back_scr[lane, pl.ds(b, MODES, stride=blocks), :] = back[:, lane * LANES:(lane + 1) * LANES]
        back = local_ref[b * MODES:(b + 1) * MODES, :] + step_decay * back
    for lane in range(groups):
        span = slice(lane * LANES, (lane + 1) * LANES)
        backs = [back_scr[lane, m * blocks:(m + 1) * blocks, :] for m in range(MODES)]
        for n in range(NODES):
            total = jnp.zeros((blocks, LANES), jnp.float32)
            for m in range(MODES):
                total = total + backs[m] * weighted_ref[n * MODES + m:n * MODES + m + 1, span]
            coef[lane, pl.ds(n, blocks, stride=NODES), :] = total
    for b in range(blocks):
        high, low = halves(
            jnp.concatenate([coef[lane, b * NODES:(b + 1) * NODES, :] for lane in range(groups)], axis=1)
        )
        far = dot32(spread_ref[...], jnp.concatenate([high, low, high], axis=0))
        rows = slice(b * BLK, (b + 1) * BLK)
        out_ref[rows, :] = (near_ref[rows, :] + far).astype(jnp.bfloat16)
        block_out(b).start()
    for b in range(blocks):
        block_out(b).wait()
    for copy in grad_copies:
        copy.wait()


def cols(rows):
    return pl.BlockSpec((rows, TILE), lambda i: (0, i))


def whole(table):
    return pl.BlockSpec(table.shape, lambda i: (0, 0))


def f32_rows(rows, channels):
    return jax.ShapeDtypeStruct((rows, channels), jnp.float32)


def cost(flops, size):
    return pl.CostEstimate(flops=int(flops), bytes_accessed=int(size), transcendentals=0)


PARAMS = pltpu.CompilerParams(vmem_limit_bytes=VMEM_LIMIT)


def in_hbm(array):
    return pltpu.with_memory_space_constraint(array, pltpu.HBM)


def call_sums(inputs, grad_out, log_rates):
    tokens, channels = inputs.shape
    blocks = tokens // BLK
    t = tables()
    consts = [jnp.asarray(t[k]) for k in ("trans_in", "trans_gr", "fold")]
    spec_rows = 2 * BLK + 2 * NODES
    far = pl.BlockSpec(memory_space=pltpu.HBM)
    near = pl.BlockSpec(memory_space=pltpu.VMEM)
    return pl.pallas_call(
        functools.partial(sums_kernel, t["nodes"], blocks),
        in_specs=[far] * 6,
        out_specs=[near, near],
        out_shape=[f32_rows(MODES * ROWS, channels), f32_rows(MODES * blocks, channels)],
        scratch_shapes=[
            pltpu.VMEM((MODES, channels), jnp.float32),
            pltpu.VMEM((tokens, channels), jnp.bfloat16),
            pltpu.VMEM((tokens, channels), jnp.bfloat16),
            pltpu.VMEM(consts[0].shape, jnp.bfloat16),
            pltpu.VMEM(consts[1].shape, jnp.bfloat16),
            pltpu.VMEM(consts[2].shape, jnp.bfloat16),
            pltpu.VMEM((PAIRS, spec_rows, channels), jnp.float32),
            pltpu.VMEM((PAIRS, spec_rows, channels), jnp.float32),
            pltpu.VMEM((NODES * MODES, channels), jnp.float32),
            pltpu.VMEM((channels // TILE, 4, NODES, TILE), jnp.float32),
            pltpu.VMEM((2 * BLK, channels), jnp.float32),
            pltpu.VMEM((channels // LANES, MODES * ROWS, LANES), jnp.float32),
            pltpu.SemaphoreType.DMA((4,)),
            pltpu.SemaphoreType.DMA((blocks,)),
            pltpu.SemaphoreType.DMA((blocks,)),
        ],
        compiler_params=PARAMS,
        cost_estimate=cost(4 * spec_rows * tokens * channels, 8 * tokens * channels),
    )(*map(in_hbm, (inputs, grad_out, log_rates, *consts)))


def call_nearby(grad_out, log_rates, residues, skip_line):
    tokens, channels = grad_out.shape
    t = tables()
    consts = [jnp.asarray(t[k]) for k in ("forward", "inverse", "lift")]
    blocks = tokens // BLK
    far = pl.BlockSpec(memory_space=pltpu.HBM)
    near = pl.BlockSpec(memory_space=pltpu.VMEM)
    return pl.pallas_call(
        functools.partial(nearby_kernel, t["nodes"], blocks),
        in_specs=[far, near, near, near, far, far, far],
        out_specs=[near, near],
        out_shape=[jax.ShapeDtypeStruct((tokens, channels), NEAR_TYPE), f32_rows(NODES * MODES, channels)],
        scratch_shapes=[
            pltpu.VMEM((tokens, channels), jnp.bfloat16),
            pltpu.VMEM(consts[0].shape, jnp.bfloat16),
            pltpu.VMEM(consts[1].shape, jnp.bfloat16),
            pltpu.VMEM(consts[2].shape, jnp.bfloat16),
            pltpu.VMEM((NODES, channels), jnp.float32),
            pltpu.VMEM((2 * BLK, channels), jnp.float32),
            pltpu.VMEM((2, 2 * BLK, channels), jnp.bfloat16),
            pltpu.SemaphoreType.DMA((3,)),
            pltpu.SemaphoreType.DMA((blocks,)),
        ],
        compiler_params=PARAMS,
        cost_estimate=cost(8 * BLK * tokens * channels, 6 * tokens * channels),
    )(in_hbm(grad_out), log_rates, residues, skip_line, *map(in_hbm, consts))


def call_scan(by_mode, tokens):
    return pl.pallas_call(
        functools.partial(scan_kernel, by_mode.shape[0], float(tokens)),
        out_shape=jax.ShapeDtypeStruct(by_mode.shape, jnp.float32),
        compiler_params=PARAMS,
    )(by_mode)


def call_finish(scaling, nearby, back, weighted, local, log_rates, residues):
    tokens, channels = nearby.shape
    blocks = tokens // BLK
    spread = jnp.asarray(tables()["spread"])
    far = pl.BlockSpec(memory_space=pltpu.HBM)
    near = pl.BlockSpec(memory_space=pltpu.VMEM)
    return pl.pallas_call(
        functools.partial(finish_kernel, blocks, scaling),
        in_specs=[near] * 7,
        out_specs=[far] * 4,
        out_shape=[
            jax.ShapeDtypeStruct((tokens, channels), jnp.bfloat16),
            f32_rows(MODES, channels),
            f32_rows(MODES, channels),
            f32_rows(1, channels),
        ],
        scratch_shapes=[
            pltpu.VMEM((tokens, channels), jnp.bfloat16),
            pltpu.VMEM((MODES, channels), jnp.float32),
            pltpu.VMEM((MODES, channels), jnp.float32),
            pltpu.VMEM((1, channels), jnp.float32),
            pltpu.VMEM((channels // LANES, MODES * ROWS, LANES), jnp.float32),
            pltpu.VMEM((channels // LANES, MODES * blocks, LANES), jnp.float32),
            pltpu.VMEM((channels // LANES, NODES * blocks, LANES), jnp.float32),
            pltpu.SemaphoreType.DMA((blocks,)),
            pltpu.SemaphoreType.DMA((3,)),
        ],
        compiler_params=PARAMS,
    )(nearby, back, weighted, local, log_rates, residues, spread)


def on_device(inputs, grad_out, residues, log_rates, skip_weight):
    tokens, channels = inputs.shape
    scaling = 1.0 / math.sqrt(tokens * lax.axis_size("ctx"))
    residues, log_rates = residues.T, log_rates.T
    summed, local = call_sums(inputs, grad_out, log_rates)
    by_mode = lax.all_to_all(
        summed.reshape(MODES, ROWS, channels), "ctx", split_axis=0, concat_axis=0, tiled=True
    )
    nearby, weighted = call_nearby(grad_out, log_rates, residues, skip_weight.reshape(1, channels))
    scanned = call_scan(by_mode, tokens)
    back = lax.all_to_all(scanned, "ctx", split_axis=0, concat_axis=0, tiled=True)
    grad_inputs, grad_residues, grad_log_rates, grad_skip = call_finish(
        scaling, nearby, back.reshape(MODES * ROWS, channels), weighted, local, log_rates, residues
    )
    return grad_inputs, grad_residues.T, grad_log_rates.T, grad_skip.reshape(channels)


def solution(mesh):
    placed = (P("ctx", "ch"), P("ctx", "ch"), P("ch", None), P("ch", None), P("ch"))
    return jax.shard_map(
        on_device,
        mesh=mesh,
        in_specs=placed,
        out_specs=(P("ctx", "ch"), P("ch", None), P("ch", None), P("ch")),
        check_vma=False,
    )
```

```python
import functools
import math

import jax
import jax.numpy as jnp
import ml_dtypes
import numpy as np
from jax import lax
from jax.experimental import pallas as pl
from jax.experimental.pallas import tpu as pltpu
from jax.sharding import PartitionSpec as P

MODES = 16
BLK = 256
NODES = 24
TILE = 256
LANES = 128
GROUPS = TILE // LANES
ROWS = 8
PAIRS = 4
SCHEDULE = ((0, 1), (2, 3), (4, 5), (6,), (7,))
NEAR_TYPE = jnp.bfloat16
VMEM_LIMIT = 24 * 1024 * 1024


def split_bf16(table):
    high = table.astype(ml_dtypes.bfloat16)
    low = (table - high.astype(np.float64)).astype(ml_dtypes.bfloat16)
    return high, low


@functools.cache
def tables():
    order = np.arange(NODES)
    angle = (2 * order + 1) * math.pi / (2 * NODES)
    nodes = 0.5 * BLK * (1 + np.cos(angle))
    spots = np.arange(BLK + 1.0)
    basis = ((-1.0) ** order * np.sin(angle)) / (spots[:, None] - nodes[None])
    basis = basis / basis.sum(axis=1, keepdims=True)
    ahead = basis[:BLK].T
    behind = basis[BLK - np.arange(BLK)].T
    phase = 2 * math.pi * (np.arange(BLK)[:, None] + 0.5) * np.arange(BLK)[None] / (2 * BLK)
    forward = np.concatenate([np.cos(phase), np.sin(phase)], axis=0)
    inverse = np.concatenate([np.cos(phase).T, -np.sin(phase).T], axis=1) / BLK
    bf16 = ml_dtypes.bfloat16
    trans_in = np.concatenate([forward.astype(bf16), *split_bf16(behind)], axis=0)
    trans_gr = np.concatenate([forward.astype(bf16), *split_bf16(ahead)], axis=0)
    fold = np.concatenate([ahead @ inverse, inverse[:1], np.zeros((7, 2 * BLK))], axis=0)
    fold_high, fold_low = split_bf16(fold)
    fold_table = np.concatenate([fold_high, fold_low], axis=0)
    lift_high, lift_low = split_bf16(forward @ ahead.T)
    lift_table = np.concatenate([lift_high, lift_high, lift_low], axis=1)
    spread_high, spread_low = split_bf16(behind.T)
    spread = np.concatenate([spread_high, spread_high, spread_low], axis=1)
    return {
        "nodes": [float(x) for x in nodes.astype(np.float32)],
        "trans_in": trans_in,
        "trans_gr": trans_gr,
        "forward": forward.astype(bf16),
        "inverse": inverse.astype(bf16),
        "fold": fold_table,
        "lift": lift_table,
        "spread": spread,
    }


def dot32(left, right):
    return jnp.dot(left, right, preferred_element_type=jnp.float32)


def halves(values):
    high = values.astype(jnp.bfloat16)
    low = (values - high.astype(jnp.float32)).astype(jnp.bfloat16)
    return high, low


def sums_kernel(nodes, blocks, in_hbm, gr_hbm, rate_hbm, tin_hbm, tgr_hbm, fold_hbm,
                out_ref, local_ref, rate_ref, in_ref, gr_ref, tin_ref, tgr_ref, fold_ref, uspec, gspec,
                mode_exp, points, cross, packed, table_sem, in_sem, gr_sem):
    channels = rate_ref.shape[1]
    tiles = channels // TILE
    spec_rows = 2 * BLK + 2 * NODES

    def tables_in():
        return [
            pltpu.make_async_copy(src, dst, table_sem.at[k])
            for k, (src, dst) in enumerate(((tin_hbm, tin_ref), (tgr_hbm, tgr_ref), (fold_hbm, fold_ref)))
        ]

    def block_in(b):
        rows = pl.ds(b * BLK, BLK)
        return (
            pltpu.make_async_copy(in_hbm.at[rows, :], in_ref.at[rows, :], in_sem.at[b]),
            pltpu.make_async_copy(gr_hbm.at[rows, :], gr_ref.at[rows, :], gr_sem.at[b]),
        )

    rate_copy = pltpu.make_async_copy(rate_hbm, rate_ref, table_sem.at[3])
    rate_copy.start()
    table_copies = tables_in()
    table_copies[0].start()
    block_copies = [block_in(b) for b in range(blocks)]
    block_copies[0][0].start()
    table_copies[1].start()
    block_copies[0][1].start()
    for b in range(1, blocks):
        block_copies[b][0].start()
        block_copies[b][1].start()
    table_copies[2].start()

    rate_copy.wait()
    rates = jnp.exp(rate_ref[...])
    step_decay = jnp.exp(rates * (-float(BLK)))
    for n in range(NODES):
        mode_exp[pl.ds(n * MODES, MODES), :] = jnp.exp(rates * (-nodes[n]))

    def lanes(c):
        return slice(c * TILE, (c + 1) * TILE)

    def transform(b):
        slot = b % PAIRS
        rows = slice(b * BLK, (b + 1) * BLK)

        def product(spec, table, data, c):
            def emit():
                spec[slot, :, lanes(c)] = dot32(table[...], data[rows, lanes(c)])

            return emit

        return [
            product(spec, table, data, c)
            for c in range(tiles)
            for spec, table, data in ((uspec, tin_ref, in_ref), (gspec, tgr_ref, gr_ref))
        ]

    def cross_rows(group, c, low, high):
        def emit():
            for j in range(low, high):
                cos_rows = slice(j * 8, j * 8 + 8)
                sin_rows = slice(BLK + j * 8, BLK + j * 8 + 8)
                real, imag = None, None
                for b in group:
                    slot = b % PAIRS
                    uc, us = uspec[slot, cos_rows, lanes(c)], uspec[slot, sin_rows, lanes(c)]
                    gc, gs = gspec[slot, cos_rows, lanes(c)], gspec[slot, sin_rows, lanes(c)]
                    re, im = gc * uc + gs * us, gc * us - gs * uc
                    real = re if real is None else real + re
                    imag = im if imag is None else imag + im
                if group[0]:
                    real = real + cross[cos_rows, lanes(c)]
                    imag = imag + cross[sin_rows, lanes(c)]
                cross[cos_rows, lanes(c)] = real
                cross[sin_rows, lanes(c)] = imag

        return emit

    def contract(c, series):
        count = len(series)
        for k, values in enumerate(series):
            points[c, k] = values
        zero = jnp.zeros((MODES, TILE), jnp.float32)
        totals, moments = [zero] * count, [zero] * count
        for n in range(NODES):
            decay = mode_exp[n * MODES:(n + 1) * MODES, lanes(c)]
            scaled = decay * nodes[n]
            for k in range(count):
                line = points[c, k, n:n + 1, :]
                totals[k] = totals[k] + decay * line
                moments[k] = moments[k] + scaled * line
        return totals, moments

    top = 2 * BLK
    mid = top + NODES
    zero = jnp.zeros((MODES, TILE), jnp.float32)
    state = [[zero, zero, zero, zero, zero, zero, zero + 1.0] for _ in range(tiles)]

    def modal(group, c):
        def emit():
            first, second, sum_in, mom_in, gsum, gmom, reach = state[c]
            series = []
            for b in group:
                for spec in (uspec, gspec):
                    slot = b % PAIRS
                    series.append(spec[slot, top:mid, lanes(c)] + spec[slot, mid:spec_rows, lanes(c)])
            totals, moments = contract(c, series)
            decay = step_decay[:, lanes(c)]
            for k, b in enumerate(group):
                u_sum, g_sum = totals[2 * k], totals[2 * k + 1]
                u_mom, g_mom = moments[2 * k], moments[2 * k + 1]
                local_ref[b * MODES:(b + 1) * MODES, lanes(c)] = g_sum
                first = first + g_sum * sum_in
                second = second + (g_mom * sum_in + g_sum * mom_in)
                gsum = gsum + reach * g_sum
                gmom = gmom + reach * (g_mom + float(BLK * b) * g_sum)
                mom_in = decay * (mom_in + float(BLK) * sum_in) + u_mom
                sum_in = decay * sum_in + u_sum
                reach = reach * decay
            state[c] = [first, second, sum_in, mom_in, gsum, gmom, reach]

        return emit

    table_copies[0].wait()
    table_copies[1].wait()
    def vector_work(group):
        work = []
        for c in range(tiles):
            work.append(cross_rows(group, c, 0, BLK // 16))
            work.append(modal(group, c))
            work.append(cross_rows(group, c, BLK // 16, BLK // 8))
        return work

    groups = SCHEDULE
    work = []
    for group in groups:
        products = []
        for b in group:
            for copy in block_copies[b]:
                copy.wait()
            products += transform(b)
        done = 0
        for k, product in enumerate(products):
            upto = (k + 1) * len(work) // len(products)
            for emit in work[done:upto]:
                emit()
            done = upto
            product()
        work = vector_work(group)
    for emit in work:
        emit()
    table_copies[2].wait()
    for c in range(tiles):
        high, low = halves(cross[:, lanes(c)])
        wide = dot32(fold_ref[...], high)
        folded = wide[:32] + wide[32:] + dot32(fold_ref[:32, :], low)
        totals, moments = contract(c, [folded[:NODES]])
        first, second, sum_in, mom_in, gsum, gmom, _ = state[c]
        skip_rows = jnp.broadcast_to(folded[NODES:NODES + 1], (MODES, TILE))
        parts = (first + totals[0], second + moments[0], sum_in, mom_in, gsum, gmom, skip_rows, rates[:, lanes(c)])
        for half in range(GROUPS):
            span = slice(half * LANES, (half + 1) * LANES)
            group = c * GROUPS + half
            for q, part in enumerate(parts):
                packed[group, pl.ds(q, MODES, stride=ROWS), :] = part[:, span]
            out_ref[:, group * LANES:(group + 1) * LANES] = packed[group]


def nearby_kernel(nodes, blocks, gr_hbm, rate_ref, res_ref, skip_ref, fwd_hbm, inv_hbm, lift_hbm,
                  near_ref, weighted_ref, gr_ref, fwd_ref, inv_ref, lift_ref, impulse, filt, response,
                  table_sem, gr_sem):
    channels = rate_ref.shape[1]
    tiles = channels // TILE

    def table_in(k):
        src, dst = ((lift_hbm, lift_ref), (fwd_hbm, fwd_ref), (inv_hbm, inv_ref))[k]
        return pltpu.make_async_copy(src, dst, table_sem.at[k])

    def block_in(b):
        rows = pl.ds(b * BLK, BLK)
        return pltpu.make_async_copy(gr_hbm.at[rows, :], gr_ref.at[rows, :], gr_sem.at[b])

    for k in range(3):
        table_in(k).start()
    for b in range(blocks):
        block_in(b).start()

    rates = jnp.exp(rate_ref[...])
    weights = 0.25 * res_ref[...] * jnp.sqrt(rates)
    for n in range(NODES):
        weighted = weights * jnp.exp(rates * (-nodes[n]))
        weighted_ref[n * MODES:(n + 1) * MODES, :] = weighted
        impulse[n:n + 1, :] = jnp.sum(weighted, axis=0, keepdims=True)
    high, low = halves(impulse[...])
    table_in(0).wait()
    filt[...] = dot32(lift_ref[...], jnp.concatenate([high, low, high], axis=0))
    skip = skip_ref[...]
    table_in(1).wait()
    table_in(2).wait()
    for b in range(blocks):
        block_in(b).wait()
        rows = slice(b * BLK, (b + 1) * BLK)
        slot = b % 2
        for c in range(tiles):
            lanes = slice(c * TILE, (c + 1) * TILE)
            spec = dot32(fwd_ref[...], gr_ref[rows, lanes])
            gc, gs = spec[:BLK], spec[BLK:]
            hc, hs = filt[:BLK, lanes], filt[BLK:, lanes]
            response[slot, :BLK, lanes] = (gc * hc + gs * hs).astype(jnp.bfloat16)
            response[slot, BLK:, lanes] = (gc * hs - gs * hc).astype(jnp.bfloat16)
        for c in range(tiles):
            lanes = slice(c * TILE, (c + 1) * TILE)
            near = dot32(inv_ref[...], response[slot, :, lanes])
            near = near + skip[:, lanes] * gr_ref[rows, lanes].astype(jnp.float32)
            near_ref[rows, lanes] = near.astype(NEAR_TYPE)


def scan_kernel(shards, span, in_ref, out_ref):
    decay = jnp.exp(in_ref[0, 7:8, :] * (-span))

    def row(d, q):
        return in_ref[d, q:q + 1, :]

    zero = jnp.zeros_like(decay)
    first, second, skip, sum_in, mom_in = zero, zero, zero, zero, zero
    for d in range(shards):
        gsum, gmom = row(d, 4), row(d, 5)
        first = first + (row(d, 0) + gsum * sum_in)
        second = second + (row(d, 1) + (gmom * sum_in + gsum * mom_in))
        skip = skip + row(d, 6)
        mom_in = decay * (mom_in + span * sum_in) + row(d, 3)
        sum_in = decay * sum_in + row(d, 2)
    width = first.shape[1] // 2

    def folded(line):
        return [line[:, :width], line[:, width:]]

    sums = folded(first) + folded(second) + folded(skip)
    back = zero
    for d in reversed(range(shards)):
        out_ref[d] = jnp.concatenate(folded(back) + sums, axis=0)
        back = row(d, 4) + decay * back


def finish_kernel(blocks, scaling, near_ref, mid_ref, weighted_ref, local_ref, rate_ref, res_ref, spread_ref,
                  out_hbm, gres_hbm, grate_hbm, gskip_hbm, out_ref, gres_ref, grate_ref, gskip_ref,
                  packed, back_scr, coef, out_sem, grad_sem):
    channels = rate_ref.shape[1]
    groups = channels // LANES

    def block_out(b):
        rows = pl.ds(b * BLK, BLK)
        return pltpu.make_async_copy(out_ref.at[rows, :], out_hbm.at[rows, :], out_sem.at[b])

    rates = jnp.exp(rate_ref[...])
    residues = res_ref[...]
    root = jnp.sqrt(rates)
    weights = 0.25 * residues * root
    step_decay = jnp.exp(rates * (-float(BLK)))
    folds = groups // 2
    for lane in range(folds):
        packed[lane] = mid_ref[:, lane * LANES:(lane + 1) * LANES]

    def picked(q):
        return jnp.concatenate(
            [
                packed[lane % folds, pl.ds(2 * q + lane // folds, MODES, stride=ROWS), :]
                for lane in range(groups)
            ],
            axis=1,
        )

    first, second = picked(1), picked(2)
    gres_ref[...] = 0.25 * root * first * scaling
    grate_ref[...] = (0.125 * residues * root * first - rates * weights * second) * scaling
    gskip_ref[...] = jnp.concatenate([mid_ref[6:7, :], mid_ref[7:8, :]], axis=1) * scaling
    grad_copies = [
        pltpu.make_async_copy(src, dst, grad_sem.at[k])
        for k, (src, dst) in enumerate(((gres_ref, gres_hbm), (grate_ref, grate_hbm), (gskip_ref, gskip_hbm)))
    ]
    for copy in grad_copies:
        copy.start()

    back = picked(0)
    for b in reversed(range(blocks)):
        for lane in range(groups):
            back_scr[lane, pl.ds(b, MODES, stride=blocks), :] = back[:, lane * LANES:(lane + 1) * LANES]
        back = local_ref[b * MODES:(b + 1) * MODES, :] + step_decay * back
    for lane in range(groups):
        span = slice(lane * LANES, (lane + 1) * LANES)
        backs = [back_scr[lane, m * blocks:(m + 1) * blocks, :] for m in range(MODES)]
        for n in range(NODES):
            total = jnp.zeros((blocks, LANES), jnp.float32)
            for m in range(MODES):
                total = total + backs[m] * weighted_ref[n * MODES + m:n * MODES + m + 1, span]
            coef[lane, pl.ds(n, blocks, stride=NODES), :] = total
    for b in range(blocks):
        high, low = halves(
            jnp.concatenate([coef[lane, b * NODES:(b + 1) * NODES, :] for lane in range(groups)], axis=1)
        )
        far = dot32(spread_ref[...], jnp.concatenate([high, low, high], axis=0))
        rows = slice(b * BLK, (b + 1) * BLK)
        out_ref[rows, :] = (near_ref[rows, :] + far).astype(jnp.bfloat16)
        block_out(b).start()
    for b in range(blocks):
        block_out(b).wait()
    for copy in grad_copies:
        copy.wait()


def cols(rows):
    return pl.BlockSpec((rows, TILE), lambda i: (0, i))


def whole(table):
    return pl.BlockSpec(table.shape, lambda i: (0, 0))


def f32_rows(rows, channels):
    return jax.ShapeDtypeStruct((rows, channels), jnp.float32)


def cost(flops, size):
    return pl.CostEstimate(flops=int(flops), bytes_accessed=int(size), transcendentals=0)


PARAMS = pltpu.CompilerParams(vmem_limit_bytes=VMEM_LIMIT)


def in_hbm(array):
    return pltpu.with_memory_space_constraint(array, pltpu.HBM)


def call_sums(inputs, grad_out, log_rates):
    tokens, channels = inputs.shape
    blocks = tokens // BLK
    t = tables()
    consts = [jnp.asarray(t[k]) for k in ("trans_in", "trans_gr", "fold")]
    spec_rows = 2 * BLK + 2 * NODES
    far = pl.BlockSpec(memory_space=pltpu.HBM)
    near = pl.BlockSpec(memory_space=pltpu.VMEM)
    return pl.pallas_call(
        functools.partial(sums_kernel, t["nodes"], blocks),
        in_specs=[far] * 6,
        out_specs=[near, near],
        out_shape=[f32_rows(MODES * ROWS, channels), f32_rows(MODES * blocks, channels)],
        scratch_shapes=[
            pltpu.VMEM((MODES, channels), jnp.float32),
            pltpu.VMEM((tokens, channels), jnp.bfloat16),
            pltpu.VMEM((tokens, channels), jnp.bfloat16),
            pltpu.VMEM(consts[0].shape, jnp.bfloat16),
            pltpu.VMEM(consts[1].shape, jnp.bfloat16),
            pltpu.VMEM(consts[2].shape, jnp.bfloat16),
            pltpu.VMEM((PAIRS, spec_rows, channels), jnp.float32),
            pltpu.VMEM((PAIRS, spec_rows, channels), jnp.float32),
            pltpu.VMEM((NODES * MODES, channels), jnp.float32),
            pltpu.VMEM((channels // TILE, 4, NODES, TILE), jnp.float32),
            pltpu.VMEM((2 * BLK, channels), jnp.float32),
            pltpu.VMEM((channels // LANES, MODES * ROWS, LANES), jnp.float32),
            pltpu.SemaphoreType.DMA((4,)),
            pltpu.SemaphoreType.DMA((blocks,)),
            pltpu.SemaphoreType.DMA((blocks,)),
        ],
        compiler_params=PARAMS,
        cost_estimate=cost(4 * spec_rows * tokens * channels, 8 * tokens * channels),
    )(*map(in_hbm, (inputs, grad_out, log_rates, *consts)))


def call_nearby(grad_out, log_rates, residues, skip_line):
    tokens, channels = grad_out.shape
    t = tables()
    consts = [jnp.asarray(t[k]) for k in ("forward", "inverse", "lift")]
    blocks = tokens // BLK
    far = pl.BlockSpec(memory_space=pltpu.HBM)
    near = pl.BlockSpec(memory_space=pltpu.VMEM)
    return pl.pallas_call(
        functools.partial(nearby_kernel, t["nodes"], blocks),
        in_specs=[far, near, near, near, far, far, far],
        out_specs=[near, near],
        out_shape=[jax.ShapeDtypeStruct((tokens, channels), NEAR_TYPE), f32_rows(NODES * MODES, channels)],
        scratch_shapes=[
            pltpu.VMEM((tokens, channels), jnp.bfloat16),
            pltpu.VMEM(consts[0].shape, jnp.bfloat16),
            pltpu.VMEM(consts[1].shape, jnp.bfloat16),
            pltpu.VMEM(consts[2].shape, jnp.bfloat16),
            pltpu.VMEM((NODES, channels), jnp.float32),
            pltpu.VMEM((2 * BLK, channels), jnp.float32),
            pltpu.VMEM((2, 2 * BLK, channels), jnp.bfloat16),
            pltpu.SemaphoreType.DMA((3,)),
            pltpu.SemaphoreType.DMA((blocks,)),
        ],
        compiler_params=PARAMS,
        cost_estimate=cost(8 * BLK * tokens * channels, 6 * tokens * channels),
    )(in_hbm(grad_out), log_rates, residues, skip_line, *map(in_hbm, consts))


def call_scan(by_mode, tokens):
    shards, rows, channels = by_mode.shape
    return pl.pallas_call(
        functools.partial(scan_kernel, shards, float(tokens)),
        out_shape=jax.ShapeDtypeStruct((shards, rows, channels // 2), jnp.float32),
        compiler_params=PARAMS,
    )(by_mode)


def call_finish(scaling, nearby, back, weighted, local, log_rates, residues):
    tokens, channels = nearby.shape
    blocks = tokens // BLK
    spread = jnp.asarray(tables()["spread"])
    far = pl.BlockSpec(memory_space=pltpu.HBM)
    near = pl.BlockSpec(memory_space=pltpu.VMEM)
    return pl.pallas_call(
        functools.partial(finish_kernel, blocks, scaling),
        in_specs=[near] * 7,
        out_specs=[far] * 4,
        out_shape=[
            jax.ShapeDtypeStruct((tokens, channels), jnp.bfloat16),
            f32_rows(MODES, channels),
            f32_rows(MODES, channels),
            f32_rows(1, channels),
        ],
        scratch_shapes=[
            pltpu.VMEM((tokens, channels), jnp.bfloat16),
            pltpu.VMEM((MODES, channels), jnp.float32),
            pltpu.VMEM((MODES, channels), jnp.float32),
            pltpu.VMEM((1, channels), jnp.float32),
            pltpu.VMEM((channels // LANES // 2, MODES * ROWS, LANES), jnp.float32),
            pltpu.VMEM((channels // LANES, MODES * blocks, LANES), jnp.float32),
            pltpu.VMEM((channels // LANES, NODES * blocks, LANES), jnp.float32),
            pltpu.SemaphoreType.DMA((blocks,)),
            pltpu.SemaphoreType.DMA((3,)),
        ],
        compiler_params=PARAMS,
    )(nearby, back, weighted, local, log_rates, residues, spread)


def on_device(inputs, grad_out, residues, log_rates, skip_weight):
    tokens, channels = inputs.shape
    scaling = 1.0 / math.sqrt(tokens * lax.axis_size("ctx"))
    residues, log_rates = residues.T, log_rates.T
    summed, local = call_sums(inputs, grad_out, log_rates)
    by_mode = lax.all_to_all(
        summed.reshape(MODES, ROWS, channels), "ctx", split_axis=0, concat_axis=0, tiled=True
    )
    nearby, weighted = call_nearby(grad_out, log_rates, residues, skip_weight.reshape(1, channels))
    scanned = call_scan(by_mode, tokens)
    back = lax.all_to_all(scanned, "ctx", split_axis=0, concat_axis=0, tiled=True)
    grad_inputs, grad_residues, grad_log_rates, grad_skip = call_finish(
        scaling, nearby, back.reshape(MODES * ROWS, channels // 2), weighted, local, log_rates, residues
    )
    return grad_inputs, grad_residues.T, grad_log_rates.T, grad_skip.reshape(channels)


def solution(mesh):
    placed = (P("ctx", "ch"), P("ctx", "ch"), P("ch", None), P("ch", None), P("ch"))
    return jax.shard_map(
        on_device,
        mesh=mesh,
        in_specs=placed,
        out_specs=(P("ctx", "ch"), P("ch", None), P("ch", None), P("ch")),
        check_vma=False,
    )
```

```python
import functools
import math

import jax
import jax.numpy as jnp
import ml_dtypes
import numpy as np
from jax import lax
from jax.experimental import pallas as pl
from jax.experimental.pallas import tpu as pltpu
from jax.sharding import PartitionSpec as P

MODES = 16
BLK = 256
NODES = 24
TILE = 256
LANES = 128
GROUPS = TILE // LANES
ROWS = 8
PAIRS = 4
SCHEDULE = ((0, 1), (2, 3), (4, 5), (6,), (7,))
NEAR_TYPE = jnp.bfloat16
VMEM_LIMIT = 24 * 1024 * 1024


def split_bf16(table):
    high = table.astype(ml_dtypes.bfloat16)
    low = (table - high.astype(np.float64)).astype(ml_dtypes.bfloat16)
    return high, low


@functools.cache
def tables():
    order = np.arange(NODES)
    angle = (2 * order + 1) * math.pi / (2 * NODES)
    nodes = 0.5 * BLK * (1 + np.cos(angle))
    spots = np.arange(BLK + 1.0)
    basis = ((-1.0) ** order * np.sin(angle)) / (spots[:, None] - nodes[None])
    basis = basis / basis.sum(axis=1, keepdims=True)
    ahead = basis[:BLK].T
    behind = basis[BLK - np.arange(BLK)].T
    phase = 2 * math.pi * (np.arange(BLK)[:, None] + 0.5) * np.arange(BLK)[None] / (2 * BLK)
    forward = np.concatenate([np.cos(phase), np.sin(phase)], axis=0)
    inverse = np.concatenate([np.cos(phase).T, -np.sin(phase).T], axis=1) / BLK
    bf16 = ml_dtypes.bfloat16
    trans_in = np.concatenate([forward.astype(bf16), *split_bf16(behind)], axis=0)
    trans_gr = np.concatenate([forward.astype(bf16), *split_bf16(ahead)], axis=0)
    fold = np.concatenate([ahead @ inverse, inverse[:1], np.zeros((7, 2 * BLK))], axis=0)
    fold_high, fold_low = split_bf16(fold)
    fold_table = np.concatenate([fold_high, fold_low], axis=0)
    lift_high, lift_low = split_bf16(forward @ ahead.T)
    lift_table = np.concatenate([lift_high, lift_high, lift_low], axis=1)
    spread_high, spread_low = split_bf16(behind.T)
    spread = np.concatenate([spread_high, spread_high, spread_low], axis=1)
    return {
        "nodes": [float(x) for x in nodes.astype(np.float32)],
        "trans_in": trans_in,
        "trans_gr": trans_gr,
        "forward": forward.astype(bf16),
        "inverse": inverse.astype(bf16),
        "fold": fold_table,
        "lift": lift_table,
        "spread": spread,
    }


def dot32(left, right):
    return jnp.dot(left, right, preferred_element_type=jnp.float32)


def halves(values):
    high = values.astype(jnp.bfloat16)
    low = (values - high.astype(jnp.float32)).astype(jnp.bfloat16)
    return high, low


def sums_kernel(nodes, blocks, in_hbm, gr_hbm, rate_hbm, tin_hbm, tgr_hbm, fold_hbm,
                out_ref, local_ref, rate_ref, in_ref, gr_ref, tin_ref, tgr_ref, fold_ref, uspec, gspec,
                mode_exp, points, cross, packed, table_sem, in_sem, gr_sem):
    channels = rate_ref.shape[1]
    tiles = channels // TILE
    spec_rows = 2 * BLK + 2 * NODES

    def tables_in():
        return [
            pltpu.make_async_copy(src, dst, table_sem.at[k])
            for k, (src, dst) in enumerate(((tin_hbm, tin_ref), (tgr_hbm, tgr_ref), (fold_hbm, fold_ref)))
        ]

    def block_in(b):
        rows = pl.ds(b * BLK, BLK)
        return (
            pltpu.make_async_copy(in_hbm.at[rows, :], in_ref.at[rows, :], in_sem.at[b]),
            pltpu.make_async_copy(gr_hbm.at[rows, :], gr_ref.at[rows, :], gr_sem.at[b]),
        )

    rate_copy = pltpu.make_async_copy(rate_hbm, rate_ref, table_sem.at[3])
    rate_copy.start()
    table_copies = tables_in()
    table_copies[0].start()
    block_copies = [block_in(b) for b in range(blocks)]
    block_copies[0][0].start()
    table_copies[1].start()
    block_copies[0][1].start()
    for b in range(1, blocks):
        block_copies[b][0].start()
        block_copies[b][1].start()
    table_copies[2].start()

    rate_copy.wait()
    rates = jnp.exp(rate_ref[...])
    step_decay = jnp.exp(rates * (-float(BLK)))
    for n in range(NODES):
        mode_exp[pl.ds(n * MODES, MODES), :] = jnp.exp(rates * (-nodes[n]))

    def lanes(c):
        return slice(c * TILE, (c + 1) * TILE)

    def transform(b):
        slot = b % PAIRS
        rows = slice(b * BLK, (b + 1) * BLK)

        def product(spec, table, data, c):
            def emit():
                spec[slot, :, lanes(c)] = dot32(table[...], data[rows, lanes(c)])

            return emit

        return [
            product(spec, table, data, c)
            for c in range(tiles)
            for spec, table, data in ((uspec, tin_ref, in_ref), (gspec, tgr_ref, gr_ref))
        ]

    def cross_rows(group, c, low, high):
        def emit():
            for j in range(low, high):
                cos_rows = slice(j * 8, j * 8 + 8)
                sin_rows = slice(BLK + j * 8, BLK + j * 8 + 8)
                real, imag = None, None
                for b in group:
                    slot = b % PAIRS
                    uc, us = uspec[slot, cos_rows, lanes(c)], uspec[slot, sin_rows, lanes(c)]
                    gc, gs = gspec[slot, cos_rows, lanes(c)], gspec[slot, sin_rows, lanes(c)]
                    re, im = gc * uc + gs * us, gc * us - gs * uc
                    real = re if real is None else real + re
                    imag = im if imag is None else imag + im
                if group[0]:
                    real = real + cross[cos_rows, lanes(c)]
                    imag = imag + cross[sin_rows, lanes(c)]
                cross[cos_rows, lanes(c)] = real
                cross[sin_rows, lanes(c)] = imag

        return emit

    def contract(c, series):
        count = len(series)
        for k, values in enumerate(series):
            points[c, k] = values
        zero = jnp.zeros((MODES, TILE), jnp.float32)
        totals, moments = [zero] * count, [zero] * count
        for n in range(NODES):
            decay = mode_exp[n * MODES:(n + 1) * MODES, lanes(c)]
            scaled = decay * nodes[n]
            for k in range(count):
                line = points[c, k, n:n + 1, :]
                totals[k] = totals[k] + decay * line
                moments[k] = moments[k] + scaled * line
        return totals, moments

    top = 2 * BLK
    mid = top + NODES
    zero = jnp.zeros((MODES, TILE), jnp.float32)
    state = [[zero, zero, zero, zero, zero, zero, zero + 1.0] for _ in range(tiles)]

    def modal(group, c):
        def emit():
            first, second, sum_in, mom_in, gsum, gmom, reach = state[c]
            series = []
            for b in group:
                for spec in (uspec, gspec):
                    slot = b % PAIRS
                    series.append(spec[slot, top:mid, lanes(c)] + spec[slot, mid:spec_rows, lanes(c)])
            totals, moments = contract(c, series)
            decay = step_decay[:, lanes(c)]
            for k, b in enumerate(group):
                u_sum, g_sum = totals[2 * k], totals[2 * k + 1]
                u_mom, g_mom = moments[2 * k], moments[2 * k + 1]
                local_ref[b * MODES:(b + 1) * MODES, lanes(c)] = g_sum
                first = first + g_sum * sum_in
                second = second + (g_mom * sum_in + g_sum * mom_in)
                gsum = gsum + reach * g_sum
                gmom = gmom + reach * (g_mom + float(BLK * b) * g_sum)
                mom_in = decay * (mom_in + float(BLK) * sum_in) + u_mom
                sum_in = decay * sum_in + u_sum
                reach = reach * decay
            state[c] = [first, second, sum_in, mom_in, gsum, gmom, reach]

        return emit

    table_copies[0].wait()
    table_copies[1].wait()
    def vector_work(group):
        work = []
        for c in range(tiles):
            work.append(cross_rows(group, c, 0, BLK // 16))
            work.append(modal(group, c))
            work.append(cross_rows(group, c, BLK // 16, BLK // 8))
        return work

    groups = SCHEDULE
    work = []
    for group in groups:
        products = []
        for b in group:
            for copy in block_copies[b]:
                copy.wait()
            products += transform(b)
        done = 0
        for k, product in enumerate(products):
            upto = (k + 1) * len(work) // len(products)
            for emit in work[done:upto]:
                emit()
            done = upto
            product()
        work = vector_work(group)
    for emit in work:
        emit()
    table_copies[2].wait()
    for c in range(tiles):
        high, low = halves(cross[:, lanes(c)])
        wide = dot32(fold_ref[...], high)
        folded = wide[:32] + wide[32:] + dot32(fold_ref[:32, :], low)
        totals, moments = contract(c, [folded[:NODES]])
        first, second, sum_in, mom_in, gsum, gmom, _ = state[c]
        skip_rows = jnp.broadcast_to(folded[NODES:NODES + 1], (MODES, TILE))
        parts = (first + totals[0], second + moments[0], sum_in, mom_in, gsum, gmom, skip_rows, zero)
        for half in range(GROUPS):
            span = slice(half * LANES, (half + 1) * LANES)
            for q, part in enumerate(parts):
                packed[half, pl.ds(2 * q + c, MODES, stride=2 * ROWS), :] = part[:, span]
    for half in range(GROUPS):
        out_ref[:, half * LANES:(half + 1) * LANES] = packed[half].astype(jnp.bfloat16)


def nearby_kernel(nodes, blocks, gr_hbm, rate_ref, res_ref, skip_ref, fwd_hbm, inv_hbm, lift_hbm,
                  near_ref, weighted_ref, gr_ref, fwd_ref, inv_ref, lift_ref, impulse, filt, response,
                  table_sem, gr_sem):
    channels = rate_ref.shape[1]
    tiles = channels // TILE

    def table_in(k):
        src, dst = ((lift_hbm, lift_ref), (fwd_hbm, fwd_ref), (inv_hbm, inv_ref))[k]
        return pltpu.make_async_copy(src, dst, table_sem.at[k])

    def block_in(b):
        rows = pl.ds(b * BLK, BLK)
        return pltpu.make_async_copy(gr_hbm.at[rows, :], gr_ref.at[rows, :], gr_sem.at[b])

    for k in range(3):
        table_in(k).start()
    for b in range(blocks):
        block_in(b).start()

    rates = jnp.exp(rate_ref[...])
    weights = 0.25 * res_ref[...] * jnp.sqrt(rates)
    for n in range(NODES):
        weighted = weights * jnp.exp(rates * (-nodes[n]))
        weighted_ref[n * MODES:(n + 1) * MODES, :] = weighted
        impulse[n:n + 1, :] = jnp.sum(weighted, axis=0, keepdims=True)
    high, low = halves(impulse[...])
    table_in(0).wait()
    filt[...] = dot32(lift_ref[...], jnp.concatenate([high, low, high], axis=0))
    skip = skip_ref[...]
    table_in(1).wait()
    table_in(2).wait()
    for b in range(blocks):
        block_in(b).wait()
        rows = slice(b * BLK, (b + 1) * BLK)
        slot = b % 2
        for c in range(tiles):
            lanes = slice(c * TILE, (c + 1) * TILE)
            spec = dot32(fwd_ref[...], gr_ref[rows, lanes])
            gc, gs = spec[:BLK], spec[BLK:]
            hc, hs = filt[:BLK, lanes], filt[BLK:, lanes]
            response[slot, :BLK, lanes] = (gc * hc + gs * hs).astype(jnp.bfloat16)
            response[slot, BLK:, lanes] = (gc * hs - gs * hc).astype(jnp.bfloat16)
        for c in range(tiles):
            lanes = slice(c * TILE, (c + 1) * TILE)
            near = dot32(inv_ref[...], response[slot, :, lanes])
            near = near + skip[:, lanes] * gr_ref[rows, lanes].astype(jnp.float32)
            near_ref[rows, lanes] = near.astype(NEAR_TYPE)


def scan_kernel(shards, span, in_ref, rate_ref, out_ref):
    line = rate_ref[pl.ds(lax.axis_index("ctx"), 1), :]
    width = line.shape[1] // 2
    rates = jnp.exp(jnp.concatenate([line[:, :width], line[:, width:]], axis=0))
    decay = jnp.exp(rates * (-span))
    zero = jnp.zeros_like(decay)
    first, second, skip, sum_in, mom_in = zero, zero, zero, zero, zero
    gsums = []
    for d in range(shards):
        rows = in_ref[d].astype(jnp.float32)
        f_part, s_part, u_sum, u_mom, gsum, gmom, k_part = [rows[2 * q:2 * q + 2] for q in range(7)]
        first = first + (f_part + gsum * sum_in)
        second = second + (s_part + (gmom * sum_in + gsum * mom_in))
        skip = skip + k_part
        mom_in = decay * (mom_in + span * sum_in) + u_mom
        sum_in = decay * sum_in + u_sum
        gsums.append(gsum)
    back = zero
    for d in reversed(range(shards)):
        out_ref[d] = jnp.concatenate([back, first, second, skip], axis=0)
        back = gsums[d] + decay * back


def finish_kernel(blocks, scaling, near_ref, mid_ref, weighted_ref, local_ref, rate_ref, res_ref, spread_ref,
                  out_hbm, gres_hbm, grate_hbm, gskip_hbm, out_ref, gres_ref, grate_ref, gskip_ref,
                  packed, back_scr, coef, out_sem, grad_sem):
    channels = rate_ref.shape[1]
    groups = channels // LANES

    def block_out(b):
        rows = pl.ds(b * BLK, BLK)
        return pltpu.make_async_copy(out_ref.at[rows, :], out_hbm.at[rows, :], out_sem.at[b])

    rates = jnp.exp(rate_ref[...])
    residues = res_ref[...]
    root = jnp.sqrt(rates)
    weights = 0.25 * residues * root
    step_decay = jnp.exp(rates * (-float(BLK)))
    folds = groups // 2
    for lane in range(folds):
        packed[lane] = mid_ref[:, lane * LANES:(lane + 1) * LANES]

    def picked(q):
        return jnp.concatenate(
            [
                packed[lane % folds, pl.ds(2 * q + lane // folds, MODES, stride=ROWS), :]
                for lane in range(groups)
            ],
            axis=1,
        )

    first, second = picked(1), picked(2)
    gres_ref[...] = 0.25 * root * first * scaling
    grate_ref[...] = (0.125 * residues * root * first - rates * weights * second) * scaling
    gskip_ref[...] = jnp.concatenate([mid_ref[6:7, :], mid_ref[7:8, :]], axis=1) * scaling
    grad_copies = [
        pltpu.make_async_copy(src, dst, grad_sem.at[k])
        for k, (src, dst) in enumerate(((gres_ref, gres_hbm), (grate_ref, grate_hbm), (gskip_ref, gskip_hbm)))
    ]
    for copy in grad_copies:
        copy.start()

    back = picked(0)
    for b in reversed(range(blocks)):
        for lane in range(groups):
            back_scr[lane, pl.ds(b, MODES, stride=blocks), :] = back[:, lane * LANES:(lane + 1) * LANES]
        back = local_ref[b * MODES:(b + 1) * MODES, :] + step_decay * back
    for lane in range(groups):
        span = slice(lane * LANES, (lane + 1) * LANES)
        backs = [back_scr[lane, m * blocks:(m + 1) * blocks, :] for m in range(MODES)]
        for n in range(NODES):
            total = jnp.zeros((blocks, LANES), jnp.float32)
            for m in range(MODES):
                total = total + backs[m] * weighted_ref[n * MODES + m:n * MODES + m + 1, span]
            coef[lane, pl.ds(n, blocks, stride=NODES), :] = total
    for b in range(blocks):
        high, low = halves(
            jnp.concatenate([coef[lane, b * NODES:(b + 1) * NODES, :] for lane in range(groups)], axis=1)
        )
        far = dot32(spread_ref[...], jnp.concatenate([high, low, high], axis=0))
        rows = slice(b * BLK, (b + 1) * BLK)
        out_ref[rows, :] = (near_ref[rows, :] + far).astype(jnp.bfloat16)
        block_out(b).start()
    for b in range(blocks):
        block_out(b).wait()
    for copy in grad_copies:
        copy.wait()


def cols(rows):
    return pl.BlockSpec((rows, TILE), lambda i: (0, i))


def whole(table):
    return pl.BlockSpec(table.shape, lambda i: (0, 0))


def f32_rows(rows, channels):
    return jax.ShapeDtypeStruct((rows, channels), jnp.float32)


def cost(flops, size):
    return pl.CostEstimate(flops=int(flops), bytes_accessed=int(size), transcendentals=0)


PARAMS = pltpu.CompilerParams(vmem_limit_bytes=VMEM_LIMIT)


def in_hbm(array):
    return pltpu.with_memory_space_constraint(array, pltpu.HBM)


def call_sums(inputs, grad_out, log_rates):
    tokens, channels = inputs.shape
    blocks = tokens // BLK
    t = tables()
    consts = [jnp.asarray(t[k]) for k in ("trans_in", "trans_gr", "fold")]
    spec_rows = 2 * BLK + 2 * NODES
    far = pl.BlockSpec(memory_space=pltpu.HBM)
    near = pl.BlockSpec(memory_space=pltpu.VMEM)
    return pl.pallas_call(
        functools.partial(sums_kernel, t["nodes"], blocks),
        in_specs=[far] * 6,
        out_specs=[near, near],
        out_shape=[
            jax.ShapeDtypeStruct((2 * MODES * ROWS, channels // 2), jnp.bfloat16),
            f32_rows(MODES * blocks, channels),
        ],
        scratch_shapes=[
            pltpu.VMEM((MODES, channels), jnp.float32),
            pltpu.VMEM((tokens, channels), jnp.bfloat16),
            pltpu.VMEM((tokens, channels), jnp.bfloat16),
            pltpu.VMEM(consts[0].shape, jnp.bfloat16),
            pltpu.VMEM(consts[1].shape, jnp.bfloat16),
            pltpu.VMEM(consts[2].shape, jnp.bfloat16),
            pltpu.VMEM((PAIRS, spec_rows, channels), jnp.float32),
            pltpu.VMEM((PAIRS, spec_rows, channels), jnp.float32),
            pltpu.VMEM((NODES * MODES, channels), jnp.float32),
            pltpu.VMEM((channels // TILE, 4, NODES, TILE), jnp.float32),
            pltpu.VMEM((2 * BLK, channels), jnp.float32),
            pltpu.VMEM((GROUPS, 2 * MODES * ROWS, LANES), jnp.float32),
            pltpu.SemaphoreType.DMA((4,)),
            pltpu.SemaphoreType.DMA((blocks,)),
            pltpu.SemaphoreType.DMA((blocks,)),
        ],
        compiler_params=PARAMS,
        cost_estimate=cost(4 * spec_rows * tokens * channels, 8 * tokens * channels),
    )(*map(in_hbm, (inputs, grad_out, log_rates, *consts)))


def call_nearby(grad_out, log_rates, residues, skip_line):
    tokens, channels = grad_out.shape
    t = tables()
    consts = [jnp.asarray(t[k]) for k in ("forward", "inverse", "lift")]
    blocks = tokens // BLK
    far = pl.BlockSpec(memory_space=pltpu.HBM)
    near = pl.BlockSpec(memory_space=pltpu.VMEM)
    return pl.pallas_call(
        functools.partial(nearby_kernel, t["nodes"], blocks),
        in_specs=[far, near, near, near, far, far, far],
        out_specs=[near, near],
        out_shape=[jax.ShapeDtypeStruct((tokens, channels), NEAR_TYPE), f32_rows(NODES * MODES, channels)],
        scratch_shapes=[
            pltpu.VMEM((tokens, channels), jnp.bfloat16),
            pltpu.VMEM(consts[0].shape, jnp.bfloat16),
            pltpu.VMEM(consts[1].shape, jnp.bfloat16),
            pltpu.VMEM(consts[2].shape, jnp.bfloat16),
            pltpu.VMEM((NODES, channels), jnp.float32),
            pltpu.VMEM((2 * BLK, channels), jnp.float32),
            pltpu.VMEM((2, 2 * BLK, channels), jnp.bfloat16),
            pltpu.SemaphoreType.DMA((3,)),
            pltpu.SemaphoreType.DMA((blocks,)),
        ],
        compiler_params=PARAMS,
        cost_estimate=cost(8 * BLK * tokens * channels, 6 * tokens * channels),
    )(in_hbm(grad_out), log_rates, residues, skip_line, *map(in_hbm, consts))


def call_scan(by_mode, tokens, log_rates):
    shards, _, width = by_mode.shape
    return pl.pallas_call(
        functools.partial(scan_kernel, shards, float(tokens)),
        out_shape=jax.ShapeDtypeStruct((shards, ROWS, width), jnp.float32),
        compiler_params=PARAMS,
    )(by_mode, log_rates)


def call_finish(scaling, nearby, back, weighted, local, log_rates, residues):
    tokens, channels = nearby.shape
    blocks = tokens // BLK
    spread = jnp.asarray(tables()["spread"])
    far = pl.BlockSpec(memory_space=pltpu.HBM)
    near = pl.BlockSpec(memory_space=pltpu.VMEM)
    return pl.pallas_call(
        functools.partial(finish_kernel, blocks, scaling),
        in_specs=[near] * 7,
        out_specs=[far] * 4,
        out_shape=[
            jax.ShapeDtypeStruct((tokens, channels), jnp.bfloat16),
            f32_rows(MODES, channels),
            f32_rows(MODES, channels),
            f32_rows(1, channels),
        ],
        scratch_shapes=[
            pltpu.VMEM((tokens, channels), jnp.bfloat16),
            pltpu.VMEM((MODES, channels), jnp.float32),
            pltpu.VMEM((MODES, channels), jnp.float32),
            pltpu.VMEM((1, channels), jnp.float32),
            pltpu.VMEM((channels // LANES // 2, MODES * ROWS, LANES), jnp.float32),
            pltpu.VMEM((channels // LANES, MODES * blocks, LANES), jnp.float32),
            pltpu.VMEM((channels // LANES, NODES * blocks, LANES), jnp.float32),
            pltpu.SemaphoreType.DMA((blocks,)),
            pltpu.SemaphoreType.DMA((3,)),
        ],
        compiler_params=PARAMS,
    )(nearby, back, weighted, local, log_rates, residues, spread)


def on_device(inputs, grad_out, residues, log_rates, skip_weight):
    tokens, channels = inputs.shape
    scaling = 1.0 / math.sqrt(tokens * lax.axis_size("ctx"))
    residues, log_rates = residues.T, log_rates.T
    summed, local = call_sums(inputs, grad_out, log_rates)
    by_mode = lax.all_to_all(
        summed.reshape(MODES, 2 * ROWS, channels // 2), "ctx", split_axis=0, concat_axis=0, tiled=True
    )
    nearby, weighted = call_nearby(grad_out, log_rates, residues, skip_weight.reshape(1, channels))
    scanned = call_scan(by_mode, tokens, log_rates)
    back = lax.all_to_all(scanned, "ctx", split_axis=0, concat_axis=0, tiled=True)
    grad_inputs, grad_residues, grad_log_rates, grad_skip = call_finish(
        scaling, nearby, back.reshape(MODES * ROWS, channels // 2), weighted, local, log_rates, residues
    )
    return grad_inputs, grad_residues.T, grad_log_rates.T, grad_skip.reshape(channels)


def solution(mesh):
    placed = (P("ctx", "ch"), P("ctx", "ch"), P("ch", None), P("ch", None), P("ch"))
    return jax.shard_map(
        on_device,
        mesh=mesh,
        in_specs=placed,
        out_specs=(P("ctx", "ch"), P("ch", None), P("ch", None), P("ch")),
        check_vma=False,
    )
```

```python
import functools
import math

import jax
import jax.numpy as jnp
import ml_dtypes
import numpy as np
from jax import lax
from jax.experimental import pallas as pl
from jax.experimental.pallas import tpu as pltpu
from jax.sharding import PartitionSpec as P

MODES = 16
BLK = 256
NODES = 24
TILE = 256
LANES = 128
GROUPS = TILE // LANES
ROWS = 8
PAIRS = 4
SCHEDULE = ((0, 1), (2, 3), (4, 5), (6,), (7,))
NEAR_TYPE = jnp.bfloat16
VMEM_LIMIT = 24 * 1024 * 1024


def split_bf16(table):
    high = table.astype(ml_dtypes.bfloat16)
    low = (table - high.astype(np.float64)).astype(ml_dtypes.bfloat16)
    return high, low


@functools.cache
def tables():
    order = np.arange(NODES)
    angle = (2 * order + 1) * math.pi / (2 * NODES)
    nodes = 0.5 * BLK * (1 + np.cos(angle))
    spots = np.arange(BLK + 1.0)
    basis = ((-1.0) ** order * np.sin(angle)) / (spots[:, None] - nodes[None])
    basis = basis / basis.sum(axis=1, keepdims=True)
    ahead = basis[:BLK].T
    behind = basis[BLK - np.arange(BLK)].T
    phase = 2 * math.pi * (np.arange(BLK)[:, None] + 0.5) * np.arange(BLK)[None] / (2 * BLK)
    forward = np.concatenate([np.cos(phase), np.sin(phase)], axis=0)
    inverse = np.concatenate([np.cos(phase).T, -np.sin(phase).T], axis=1) / BLK
    bf16 = ml_dtypes.bfloat16
    trans_in = np.concatenate([forward.astype(bf16), *split_bf16(behind)], axis=0)
    trans_gr = np.concatenate([forward.astype(bf16), *split_bf16(ahead)], axis=0)
    fold = np.concatenate([ahead @ inverse, inverse[:1], np.zeros((7, 2 * BLK))], axis=0)
    fold_high, fold_low = split_bf16(fold)
    fold_table = np.concatenate([fold_high, fold_low], axis=0)
    lift_high, lift_low = split_bf16(forward @ ahead.T)
    lift_table = np.concatenate([lift_high, lift_high, lift_low], axis=1)
    spread_high, spread_low = split_bf16(behind.T)
    spread = np.concatenate([spread_high, spread_high, spread_low], axis=1)
    return {
        "nodes": [float(x) for x in nodes.astype(np.float32)],
        "trans_in": trans_in,
        "trans_gr": trans_gr,
        "forward": forward.astype(bf16),
        "inverse": inverse.astype(bf16),
        "fold": fold_table,
        "lift": lift_table,
        "spread": spread,
    }


def dot32(left, right):
    return jnp.dot(left, right, preferred_element_type=jnp.float32)


def halves(values):
    high = values.astype(jnp.bfloat16)
    low = (values - high.astype(jnp.float32)).astype(jnp.bfloat16)
    return high, low


def sums_kernel(nodes, blocks, in_hbm, gr_hbm, rate_hbm, tin_hbm, tgr_hbm, fold_hbm,
                out_ref, local_ref, rate_ref, in_ref, gr_ref, tin_ref, tgr_ref, fold_ref, uspec, gspec,
                mode_exp, points, cross, packed, table_sem, in_sem, gr_sem):
    channels = rate_ref.shape[1]
    tiles = channels // TILE
    spec_rows = 2 * BLK + 2 * NODES

    def tables_in():
        return [
            pltpu.make_async_copy(src, dst, table_sem.at[k])
            for k, (src, dst) in enumerate(((tin_hbm, tin_ref), (tgr_hbm, tgr_ref), (fold_hbm, fold_ref)))
        ]

    def block_in(b):
        rows = pl.ds(b * BLK, BLK)
        return (
            pltpu.make_async_copy(in_hbm.at[rows, :], in_ref.at[rows, :], in_sem.at[b]),
            pltpu.make_async_copy(gr_hbm.at[rows, :], gr_ref.at[rows, :], gr_sem.at[b]),
        )

    rate_copy = pltpu.make_async_copy(rate_hbm, rate_ref, table_sem.at[3])
    rate_copy.start()
    table_copies = tables_in()
    table_copies[0].start()
    block_copies = [block_in(b) for b in range(blocks)]
    block_copies[0][0].start()
    table_copies[1].start()
    block_copies[0][1].start()
    for b in range(1, blocks):
        block_copies[b][0].start()
        block_copies[b][1].start()
    table_copies[2].start()

    rate_copy.wait()
    rates = jnp.exp(rate_ref[...])
    step_decay = jnp.exp(rates * (-float(BLK)))

    def decays(low, high):
        def emit():
            for n in range(low, high):
                mode_exp[n * MODES:(n + 1) * MODES, :] = jnp.exp(rates * (-nodes[n]))

        return emit


    def lanes(c):
        return slice(c * TILE, (c + 1) * TILE)

    def transform(b):
        slot = b % PAIRS
        rows = slice(b * BLK, (b + 1) * BLK)

        def product(spec, table, data, c):
            def emit():
                spec[slot, :, lanes(c)] = dot32(table[...], data[rows, lanes(c)])

            return emit

        return [
            product(spec, table, data, c)
            for c in range(tiles)
            for spec, table, data in ((uspec, tin_ref, in_ref), (gspec, tgr_ref, gr_ref))
        ]

    def cross_rows(group, c, low, high):
        def emit():
            for j in range(low, high):
                cos_rows = slice(j * 8, j * 8 + 8)
                sin_rows = slice(BLK + j * 8, BLK + j * 8 + 8)
                real, imag = None, None
                for b in group:
                    slot = b % PAIRS
                    uc, us = uspec[slot, cos_rows, lanes(c)], uspec[slot, sin_rows, lanes(c)]
                    gc, gs = gspec[slot, cos_rows, lanes(c)], gspec[slot, sin_rows, lanes(c)]
                    re, im = gc * uc + gs * us, gc * us - gs * uc
                    real = re if real is None else real + re
                    imag = im if imag is None else imag + im
                if group[0]:
                    real = real + cross[cos_rows, lanes(c)]
                    imag = imag + cross[sin_rows, lanes(c)]
                cross[cos_rows, lanes(c)] = real
                cross[sin_rows, lanes(c)] = imag

        return emit

    def contract(c, series):
        count = len(series)
        for k, values in enumerate(series):
            points[c, k] = values
        zero = jnp.zeros((MODES, TILE), jnp.float32)
        totals, moments = [zero] * count, [zero] * count
        for n in range(NODES):
            decay = mode_exp[n * MODES:(n + 1) * MODES, lanes(c)]
            scaled = decay * nodes[n]
            for k in range(count):
                line = points[c, k, n:n + 1, :]
                totals[k] = totals[k] + decay * line
                moments[k] = moments[k] + scaled * line
        return totals, moments

    top = 2 * BLK
    mid = top + NODES
    zero = jnp.zeros((MODES, TILE), jnp.float32)
    state = [[zero, zero, zero, zero, zero, zero, zero + 1.0] for _ in range(tiles)]

    def modal(group, c):
        def emit():
            first, second, sum_in, mom_in, gsum, gmom, reach = state[c]
            series = []
            for b in group:
                for spec in (uspec, gspec):
                    slot = b % PAIRS
                    series.append(spec[slot, top:mid, lanes(c)] + spec[slot, mid:spec_rows, lanes(c)])
            totals, moments = contract(c, series)
            decay = step_decay[:, lanes(c)]
            for k, b in enumerate(group):
                u_sum, g_sum = totals[2 * k], totals[2 * k + 1]
                u_mom, g_mom = moments[2 * k], moments[2 * k + 1]
                local_ref[b * MODES:(b + 1) * MODES, lanes(c)] = g_sum
                first = first + g_sum * sum_in
                second = second + (g_mom * sum_in + g_sum * mom_in)
                gsum = gsum + reach * g_sum
                gmom = gmom + reach * (g_mom + float(BLK * b) * g_sum)
                mom_in = decay * (mom_in + float(BLK) * sum_in) + u_mom
                sum_in = decay * sum_in + u_sum
                reach = reach * decay
            state[c] = [first, second, sum_in, mom_in, gsum, gmom, reach]

        return emit

    table_copies[0].wait()
    table_copies[1].wait()
    def vector_work(group):
        work = []
        for c in range(tiles):
            work.append(cross_rows(group, c, 0, BLK // 16))
            work.append(modal(group, c))
            work.append(cross_rows(group, c, BLK // 16, BLK // 8))
        return work

    groups = SCHEDULE
    work = [decays(n, n + 3) for n in range(0, NODES, 3)]
    for group in groups:
        products = []
        for b in group:
            for copy in block_copies[b]:
                copy.wait()
            products += transform(b)
        done = 0
        for k, product in enumerate(products):
            upto = (k + 1) * len(work) // len(products)
            for emit in work[done:upto]:
                emit()
            done = upto
            product()
        work = vector_work(group)
    for emit in work:
        emit()
    table_copies[2].wait()
    for c in range(tiles):
        high, low = halves(cross[:, lanes(c)])
        wide = dot32(fold_ref[...], high)
        folded = wide[:32] + wide[32:] + dot32(fold_ref[:32, :], low)
        totals, moments = contract(c, [folded[:NODES]])
        first, second, sum_in, mom_in, gsum, gmom, _ = state[c]
        skip_rows = jnp.broadcast_to(folded[NODES:NODES + 1], (MODES, TILE))
        parts = (first + totals[0], second + moments[0], sum_in, mom_in, gsum, gmom, skip_rows, zero)
        for half in range(GROUPS):
            span = slice(half * LANES, (half + 1) * LANES)
            for q, part in enumerate(parts):
                packed[half, pl.ds(2 * q + c, MODES, stride=2 * ROWS), :] = part[:, span]
    for half in range(GROUPS):
        out_ref[:, half * LANES:(half + 1) * LANES] = packed[half].astype(jnp.bfloat16)


def nearby_kernel(nodes, blocks, gr_hbm, rate_ref, res_ref, skip_ref, fwd_hbm, inv_hbm, lift_hbm,
                  near_ref, weighted_ref, gr_ref, fwd_ref, inv_ref, lift_ref, impulse, filt, response,
                  table_sem, gr_sem):
    channels = rate_ref.shape[1]
    tiles = channels // TILE

    def table_in(k):
        src, dst = ((lift_hbm, lift_ref), (fwd_hbm, fwd_ref), (inv_hbm, inv_ref))[k]
        return pltpu.make_async_copy(src, dst, table_sem.at[k])

    def block_in(b):
        rows = pl.ds(b * BLK, BLK)
        return pltpu.make_async_copy(gr_hbm.at[rows, :], gr_ref.at[rows, :], gr_sem.at[b])

    for k in range(3):
        table_in(k).start()
    for b in range(blocks):
        block_in(b).start()

    rates = jnp.exp(rate_ref[...])
    weights = 0.25 * res_ref[...] * jnp.sqrt(rates)
    for n in range(NODES):
        weighted = weights * jnp.exp(rates * (-nodes[n]))
        weighted_ref[n * MODES:(n + 1) * MODES, :] = weighted
        impulse[n:n + 1, :] = jnp.sum(weighted, axis=0, keepdims=True)
    high, low = halves(impulse[...])
    table_in(0).wait()
    filt[...] = dot32(lift_ref[...], jnp.concatenate([high, low, high], axis=0))
    skip = skip_ref[...]
    table_in(1).wait()
    table_in(2).wait()
    for b in range(blocks):
        block_in(b).wait()
        rows = slice(b * BLK, (b + 1) * BLK)
        slot = b % 2
        for c in range(tiles):
            lanes = slice(c * TILE, (c + 1) * TILE)
            spec = dot32(fwd_ref[...], gr_ref[rows, lanes])
            gc, gs = spec[:BLK], spec[BLK:]
            hc, hs = filt[:BLK, lanes], filt[BLK:, lanes]
            response[slot, :BLK, lanes] = (gc * hc + gs * hs).astype(jnp.bfloat16)
            response[slot, BLK:, lanes] = (gc * hs - gs * hc).astype(jnp.bfloat16)
        for c in range(tiles):
            lanes = slice(c * TILE, (c + 1) * TILE)
            near = dot32(inv_ref[...], response[slot, :, lanes])
            near = near + skip[:, lanes] * gr_ref[rows, lanes].astype(jnp.float32)
            near_ref[rows, lanes] = near.astype(NEAR_TYPE)


def scan_kernel(shards, span, in_ref, rate_ref, out_ref):
    line = rate_ref[pl.ds(lax.axis_index("ctx"), 1), :]
    width = line.shape[1] // 2
    rates = jnp.exp(jnp.concatenate([line[:, :width], line[:, width:]], axis=0))
    decay = jnp.exp(rates * (-span))
    zero = jnp.zeros_like(decay)
    first, second, skip, sum_in, mom_in = zero, zero, zero, zero, zero
    gsums = []
    for d in range(shards):
        rows = in_ref[d].astype(jnp.float32)
        f_part, s_part, u_sum, u_mom, gsum, gmom, k_part = [rows[2 * q:2 * q + 2] for q in range(7)]
        first = first + (f_part + gsum * sum_in)
        second = second + (s_part + (gmom * sum_in + gsum * mom_in))
        skip = skip + k_part
        mom_in = decay * (mom_in + span * sum_in) + u_mom
        sum_in = decay * sum_in + u_sum
        gsums.append(gsum)
    back = zero
    for d in reversed(range(shards)):
        out_ref[d] = jnp.concatenate([back, first, second, skip], axis=0)
        back = gsums[d] + decay * back


def finish_kernel(blocks, scaling, near_ref, mid_ref, weighted_ref, local_ref, rate_ref, res_ref, spread_ref,
                  out_hbm, gres_hbm, grate_hbm, gskip_hbm, out_ref, gres_ref, grate_ref, gskip_ref,
                  packed, back_scr, coef, out_sem, grad_sem):
    channels = rate_ref.shape[1]
    groups = channels // LANES

    def block_out(b):
        rows = pl.ds(b * BLK, BLK)
        return pltpu.make_async_copy(out_ref.at[rows, :], out_hbm.at[rows, :], out_sem.at[b])

    rates = jnp.exp(rate_ref[...])
    residues = res_ref[...]
    root = jnp.sqrt(rates)
    weights = 0.25 * residues * root
    step_decay = jnp.exp(rates * (-float(BLK)))
    folds = groups // 2
    for lane in range(folds):
        packed[lane] = mid_ref[:, lane * LANES:(lane + 1) * LANES]

    def picked(q):
        return jnp.concatenate(
            [
                packed[lane % folds, pl.ds(2 * q + lane // folds, MODES, stride=ROWS), :]
                for lane in range(groups)
            ],
            axis=1,
        )

    first, second = picked(1), picked(2)
    gres_ref[...] = 0.25 * root * first * scaling
    grate_ref[...] = (0.125 * residues * root * first - rates * weights * second) * scaling
    gskip_ref[...] = jnp.concatenate([mid_ref[6:7, :], mid_ref[7:8, :]], axis=1) * scaling
    grad_copies = [
        pltpu.make_async_copy(src, dst, grad_sem.at[k])
        for k, (src, dst) in enumerate(((gres_ref, gres_hbm), (grate_ref, grate_hbm), (gskip_ref, gskip_hbm)))
    ]
    for copy in grad_copies:
        copy.start()

    back = picked(0)
    for b in reversed(range(blocks)):
        for lane in range(groups):
            back_scr[lane, pl.ds(b, MODES, stride=blocks), :] = back[:, lane * LANES:(lane + 1) * LANES]
        back = local_ref[b * MODES:(b + 1) * MODES, :] + step_decay * back
    for lane in range(groups):
        span = slice(lane * LANES, (lane + 1) * LANES)
        backs = [back_scr[lane, m * blocks:(m + 1) * blocks, :] for m in range(MODES)]
        for n in range(NODES):
            total = jnp.zeros((blocks, LANES), jnp.float32)
            for m in range(MODES):
                total = total + backs[m] * weighted_ref[n * MODES + m:n * MODES + m + 1, span]
            coef[lane, pl.ds(n, blocks, stride=NODES), :] = total
    for b in range(blocks):
        high, low = halves(
            jnp.concatenate([coef[lane, b * NODES:(b + 1) * NODES, :] for lane in range(groups)], axis=1)
        )
        far = dot32(spread_ref[...], jnp.concatenate([high, low, high], axis=0))
        rows = slice(b * BLK, (b + 1) * BLK)
        out_ref[rows, :] = (near_ref[rows, :] + far).astype(jnp.bfloat16)
        block_out(b).start()
    for b in range(blocks):
        block_out(b).wait()
    for copy in grad_copies:
        copy.wait()


def cols(rows):
    return pl.BlockSpec((rows, TILE), lambda i: (0, i))


def whole(table):
    return pl.BlockSpec(table.shape, lambda i: (0, 0))


def f32_rows(rows, channels):
    return jax.ShapeDtypeStruct((rows, channels), jnp.float32)


def cost(flops, size):
    return pl.CostEstimate(flops=int(flops), bytes_accessed=int(size), transcendentals=0)


PARAMS = pltpu.CompilerParams(vmem_limit_bytes=VMEM_LIMIT)


def in_hbm(array):
    return pltpu.with_memory_space_constraint(array, pltpu.HBM)


def call_sums(inputs, grad_out, log_rates):
    tokens, channels = inputs.shape
    blocks = tokens // BLK
    t = tables()
    consts = [jnp.asarray(t[k]) for k in ("trans_in", "trans_gr", "fold")]
    spec_rows = 2 * BLK + 2 * NODES
    far = pl.BlockSpec(memory_space=pltpu.HBM)
    near = pl.BlockSpec(memory_space=pltpu.VMEM)
    return pl.pallas_call(
        functools.partial(sums_kernel, t["nodes"], blocks),
        in_specs=[far] * 6,
        out_specs=[near, near],
        out_shape=[
            jax.ShapeDtypeStruct((2 * MODES * ROWS, channels // 2), jnp.bfloat16),
            f32_rows(MODES * blocks, channels),
        ],
        scratch_shapes=[
            pltpu.VMEM((MODES, channels), jnp.float32),
            pltpu.VMEM((tokens, channels), jnp.bfloat16),
            pltpu.VMEM((tokens, channels), jnp.bfloat16),
            pltpu.VMEM(consts[0].shape, jnp.bfloat16),
            pltpu.VMEM(consts[1].shape, jnp.bfloat16),
            pltpu.VMEM(consts[2].shape, jnp.bfloat16),
            pltpu.VMEM((PAIRS, spec_rows, channels), jnp.float32),
            pltpu.VMEM((PAIRS, spec_rows, channels), jnp.float32),
            pltpu.VMEM((NODES * MODES, channels), jnp.float32),
            pltpu.VMEM((channels // TILE, 4, NODES, TILE), jnp.float32),
            pltpu.VMEM((2 * BLK, channels), jnp.float32),
            pltpu.VMEM((GROUPS, 2 * MODES * ROWS, LANES), jnp.float32),
            pltpu.SemaphoreType.DMA((4,)),
            pltpu.SemaphoreType.DMA((blocks,)),
            pltpu.SemaphoreType.DMA((blocks,)),
        ],
        compiler_params=PARAMS,
        cost_estimate=cost(4 * spec_rows * tokens * channels, 8 * tokens * channels),
    )(*map(in_hbm, (inputs, grad_out, log_rates, *consts)))


def call_nearby(grad_out, log_rates, residues, skip_line):
    tokens, channels = grad_out.shape
    t = tables()
    consts = [jnp.asarray(t[k]) for k in ("forward", "inverse", "lift")]
    blocks = tokens // BLK
    far = pl.BlockSpec(memory_space=pltpu.HBM)
    near = pl.BlockSpec(memory_space=pltpu.VMEM)
    return pl.pallas_call(
        functools.partial(nearby_kernel, t["nodes"], blocks),
        in_specs=[far, near, near, near, far, far, far],
        out_specs=[near, near],
        out_shape=[jax.ShapeDtypeStruct((tokens, channels), NEAR_TYPE), f32_rows(NODES * MODES, channels)],
        scratch_shapes=[
            pltpu.VMEM((tokens, channels), jnp.bfloat16),
            pltpu.VMEM(consts[0].shape, jnp.bfloat16),
            pltpu.VMEM(consts[1].shape, jnp.bfloat16),
            pltpu.VMEM(consts[2].shape, jnp.bfloat16),
            pltpu.VMEM((NODES, channels), jnp.float32),
            pltpu.VMEM((2 * BLK, channels), jnp.float32),
            pltpu.VMEM((2, 2 * BLK, channels), jnp.bfloat16),
            pltpu.SemaphoreType.DMA((3,)),
            pltpu.SemaphoreType.DMA((blocks,)),
        ],
        compiler_params=PARAMS,
        cost_estimate=cost(8 * BLK * tokens * channels, 6 * tokens * channels),
    )(in_hbm(grad_out), log_rates, residues, skip_line, *map(in_hbm, consts))


def call_scan(by_mode, tokens, log_rates):
    shards, _, width = by_mode.shape
    return pl.pallas_call(
        functools.partial(scan_kernel, shards, float(tokens)),
        out_shape=jax.ShapeDtypeStruct((shards, ROWS, width), jnp.float32),
        compiler_params=PARAMS,
    )(by_mode, log_rates)


def call_finish(scaling, nearby, back, weighted, local, log_rates, residues):
    tokens, channels = nearby.shape
    blocks = tokens // BLK
    spread = jnp.asarray(tables()["spread"])
    far = pl.BlockSpec(memory_space=pltpu.HBM)
    near = pl.BlockSpec(memory_space=pltpu.VMEM)
    return pl.pallas_call(
        functools.partial(finish_kernel, blocks, scaling),
        in_specs=[near] * 7,
        out_specs=[far] * 4,
        out_shape=[
            jax.ShapeDtypeStruct((tokens, channels), jnp.bfloat16),
            f32_rows(MODES, channels),
            f32_rows(MODES, channels),
            f32_rows(1, channels),
        ],
        scratch_shapes=[
            pltpu.VMEM((tokens, channels), jnp.bfloat16),
            pltpu.VMEM((MODES, channels), jnp.float32),
            pltpu.VMEM((MODES, channels), jnp.float32),
            pltpu.VMEM((1, channels), jnp.float32),
            pltpu.VMEM((channels // LANES // 2, MODES * ROWS, LANES), jnp.float32),
            pltpu.VMEM((channels // LANES, MODES * blocks, LANES), jnp.float32),
            pltpu.VMEM((channels // LANES, NODES * blocks, LANES), jnp.float32),
            pltpu.SemaphoreType.DMA((blocks,)),
            pltpu.SemaphoreType.DMA((3,)),
        ],
        compiler_params=PARAMS,
    )(nearby, back, weighted, local, log_rates, residues, spread)


def on_device(inputs, grad_out, residues, log_rates, skip_weight):
    tokens, channels = inputs.shape
    scaling = 1.0 / math.sqrt(tokens * lax.axis_size("ctx"))
    residues, log_rates = residues.T, log_rates.T
    summed, local = call_sums(inputs, grad_out, log_rates)
    by_mode = lax.all_to_all(
        summed.reshape(MODES, 2 * ROWS, channels // 2), "ctx", split_axis=0, concat_axis=0, tiled=True
    )
    nearby, weighted = call_nearby(grad_out, log_rates, residues, skip_weight.reshape(1, channels))
    scanned = call_scan(by_mode, tokens, log_rates)
    back = lax.all_to_all(scanned, "ctx", split_axis=0, concat_axis=0, tiled=True)
    grad_inputs, grad_residues, grad_log_rates, grad_skip = call_finish(
        scaling, nearby, back.reshape(MODES * ROWS, channels // 2), weighted, local, log_rates, residues
    )
    return grad_inputs, grad_residues.T, grad_log_rates.T, grad_skip.reshape(channels)


def solution(mesh):
    placed = (P("ctx", "ch"), P("ctx", "ch"), P("ch", None), P("ch", None), P("ch"))
    return jax.shard_map(
        on_device,
        mesh=mesh,
        in_specs=placed,
        out_specs=(P("ctx", "ch"), P("ch", None), P("ch", None), P("ch")),
        check_vma=False,
    )
```
